32 devices in a mesh: pop: 8 (over z, core), mp: 4 (over y, x).
Axes of the slice: x: 2, y: 2, z: 4, core: 2. Of those that a mesh axis runs over, the one named last changes fastest.
Arguments:
- prompts: bfloat16 [32, 128, 4096], P('pop'), may hold values from -9 to 9
- gate_weight: bfloat16 [4096, 8192], P('pop', 'mp'), may hold values from -0.09375 to 0.09375
- up_weight: bfloat16 [4096, 8192], P('pop', 'mp'), may hold values from -0.09375 to 0.09375
- reward_head: bfloat16 [8192], P('mp'), may hold values from -0.0625 to 0.0625
- member_seeds: int32 [32], P('pop'), may hold values from 0 to 1073741823
- counters: int32 [32], P('pop'), may hold values from 0 to 65535
- member_ranks: int32 [32], P('pop'), may hold values from 0 to 31, each once
Outputs:
- new_gate: bfloat16 [4096, 8192], P('pop', 'mp')
- new_up: bfloat16 [4096, 8192], P('pop', 'mp')
- scores: float32 [32], P('pop')
The draws below stay inside these ranges and needn't reach their ends.
All inputs are finite; a program needn't handle non-finite values.
Results may differ from the reference program's by a relative error of at most 0.014.
Values may be sent and summed in bfloat16 or wider, within the bound.
No kernel may reach another device: no remote copies, remote signals or barrier semaphores. Data moves between devices by JAX's collectives and lax.ppermute only.
A program may use at most 128 MiB of HBM per device.

```python
import jax
import jax.numpy as jnp
from jax import lax

D = 4096
HID = 8192
SEQ = 128
MEMBERS = 32


def draw_prompts(key, part):
    member_pos = jnp.arange(MEMBERS, dtype=jnp.float32) / max(MEMBERS - 1, 1)
    sample = jnp.clip(jax.random.normal(key, (MEMBERS, SEQ, D), jnp.float32), -6.0, 6.0)
    scaling = 0.5 + member_pos
    return (sample * scaling[:, None, None]).astype(jnp.bfloat16)


def plant(result, key, low, high):
    longest = result.shape.index(max(result.shape))
    spots = []
    for shift in (0, 1):
        where = [jax.random.randint(jax.random.fold_in(key, axis), (), 0, length) for axis, length in enumerate(result.shape)]
        where[longest] = (where[longest] + shift) % result.shape[longest]
        spots.append(tuple(where))
    return result.at[spots[0]].set(low).at[spots[1]].set(high)


def block_scale(own_key, extent, pieces, smallest, largest):
    factor_of, own = 1.0, jax.random.fold_in(own_key, 6)
    for axis_at, blocks in pieces:
        steps = jnp.exp(jax.random.uniform(jax.random.fold_in(own, axis_at), (blocks,), jnp.float32, smallest / len(pieces), largest / len(pieces)))
        factor_of = factor_of * jnp.repeat(steps, extent[axis_at] // blocks).reshape([-1 if axis == axis_at else 1 for axis in range(len(extent))])
    return factor_of


def bell_draw(rng, extent, width, most, pieces=(), kind=jnp.bfloat16):
    result = width * jax.random.normal(rng, extent, jnp.float32)
    if pieces:
        result = result * block_scale(rng, extent, pieces, -0.22, 0.18)
    return jnp.clip(result, -most, most).astype(kind)


def setup_inputs(seed: int = 0) -> dict:
    keys = jax.random.split(jax.random.key(seed), 8)
    prompts = draw_prompts(jax.random.fold_in(keys[7], 71), 0)
    gate_weight = bell_draw(keys[1], (D, HID), D ** -0.5, 0.09375, ((0, 8), (1, 4)))
    up_weight = bell_draw(keys[2], (D, HID), D ** -0.5, 0.09375, ((0, 8), (1, 4)))
    reward_head = bell_draw(keys[3], (HID,), HID ** -0.5, 0.0625, ((0, 4),))
    member_seeds = plant(jax.random.randint(keys[4], (MEMBERS,), 0, 1073741824), jax.random.fold_in(keys[4], 1), 0, 1073741823).astype(jnp.int32)
    counters = plant(jax.random.randint(keys[5], (MEMBERS,), 0, 65536), jax.random.fold_in(keys[5], 1), 0, 65535).astype(jnp.int32)
    member_ranks = jax.random.permutation(keys[6], MEMBERS).astype(jnp.int32)
    return {"prompts": prompts, "gate_weight": gate_weight, "up_weight": up_weight, "reward_head": reward_head, "member_seeds": member_seeds, "counters": counters, "member_ranks": member_ranks}


sigma_perturb = 0.004
learn_rate = 0.0016

def shift_down(number, amount):
    return lax.shift_right_logical(number, jnp.full_like(number, amount))

def mix_bits(number):
    number = number ^ shift_down(number, 16)
    number = number * 2146121005
    number = number ^ shift_down(number, 15)
    number = number * -2073254261
    return number ^ shift_down(number, 16)

def factor_rows(seed_list, counter_list, slot, positions):
    anchor = mix_bits(seed_list * 1103515245 + mix_bits(counter_list * 668265263 + slot * 374761393))
    hashed = mix_bits(anchor[:, None] + positions[None, :] * -1640531535)
    uniform_part = shift_down(hashed, 8).astype(jnp.float32) * (1.0 / 16777216.0)
    return (2.0 * uniform_part - 1.0 + 1.0 / 16777216.0) * 1.7320508075688772

def reference(prompts, gate_weight, up_weight, reward_head, member_seeds, counters, member_ranks):
    fitness = (member_ranks.astype(jnp.float32) + 0.5) / MEMBERS - 0.5
    scaling = learn_rate / (MEMBERS * sigma_perturb)
    row_index = jnp.arange(D, dtype=jnp.int32)
    col_index = jnp.arange(HID, dtype=jnp.int32)

    def updated(weight, slot):
        left_factor = (factor_rows(member_seeds, counters, slot, row_index) * fitness[:, None]).astype(jnp.bfloat16)
        right_factor = factor_rows(member_seeds, counters, slot + 1, col_index).astype(jnp.bfloat16)
        update_term = scaling * jnp.dot(left_factor.T, right_factor, preferred_element_type=jnp.float32)
        return (weight.astype(jnp.float32) + update_term).astype(jnp.bfloat16)
    new_gate = updated(gate_weight, 0)
    new_up = updated(up_weight, 2)
    later = counters + 1

    def member(inputs):
        sample, seed_one, counter_one = inputs
        seed_row = seed_one[None]
        counter_row = counter_one[None]
        gate_vec = factor_rows(seed_row, counter_row, 0, row_index)[0].astype(jnp.bfloat16)
        gate_col = factor_rows(seed_row, counter_row, 1, col_index)[0]
        up_vec = factor_rows(seed_row, counter_row, 2, row_index)[0].astype(jnp.bfloat16)
        up_col = factor_rows(seed_row, counter_row, 3, col_index)[0]
        gate_value = jnp.dot(sample, new_gate, preferred_element_type=jnp.float32) + sigma_perturb * jnp.dot(sample, gate_vec, preferred_element_type=jnp.float32)[:, None] * gate_col[None, :]
        up_value = jnp.dot(sample, new_up, preferred_element_type=jnp.float32) + sigma_perturb * jnp.dot(sample, up_vec, preferred_element_type=jnp.float32)[:, None] * up_col[None, :]
        hidden = (jax.nn.silu(gate_value) * up_value).astype(jnp.bfloat16)
        return jnp.sum(jnp.dot(hidden, reward_head, preferred_element_type=jnp.float32)) / SEQ
    rewards = lax.map(member, (prompts, member_seeds, later))
    reward_mean = jnp.mean(rewards)
    reward_var = jnp.mean((rewards - reward_mean) ** 2)
    scores = (rewards - reward_mean) / jnp.sqrt(reward_var + 1e-05)
    return (new_gate, new_up, scores)
```

```python
import jax
import jax.numpy as jnp
from jax import lax
from jax.experimental import pallas as pl
from jax.experimental.pallas import tpu as pltpu
from jax.sharding import PartitionSpec as P

sigma_perturb = 0.004
learn_rate = 0.0016
AXES = ("pop", "mp")
CORES = 2


def shift_down(number, amount):
    return lax.shift_right_logical(number, jnp.full_like(number, amount))


def mix_bits(number):
    number = number ^ shift_down(number, 16)
    number = number * 2146121005
    number = number ^ shift_down(number, 15)
    number = number * -2073254261
    return number ^ shift_down(number, 16)


def factor_rows(seed_list, counter_list, slot, positions):
    anchor = mix_bits(
        seed_list * 1103515245 + mix_bits(counter_list * 668265263 + slot * 374761393)
    )
    hashed = mix_bits(anchor[:, None] + positions[None, :] * -1640531535)
    uniform_part = shift_down(hashed, 8).astype(jnp.float32) * (1.0 / 16777216.0)
    return (2.0 * uniform_part - 1.0 + 1.0 / 16777216.0) * 1.7320508075688772


def fresh_weights(gate_weight, up_weight, seeds, counters, ranks, row_start, column_ids):
    members_all = seeds.shape[0]
    fitness = (ranks.astype(jnp.float32) + 0.5) / members_all - 0.5
    scaling = learn_rate / (members_all * sigma_perturb)
    row_ids = row_start + jnp.arange(gate_weight.shape[0], dtype=jnp.int32)

    def fresh(weight, slot):
        right = factor_rows(seeds, counters, slot + 1, column_ids).astype(jnp.bfloat16)
        left = (factor_rows(seeds, counters, slot, row_ids) * fitness[:, None]).astype(jnp.bfloat16)
        update = scaling * jnp.dot(left.T, right, preferred_element_type=jnp.float32)
        return (weight.astype(jnp.float32) + update).astype(jnp.bfloat16)

    return fresh(gate_weight, 0), fresh(up_weight, 2)


def normalized(rewards):
    reward_mean = jnp.mean(rewards)
    reward_var = jnp.mean((rewards - reward_mean) ** 2)
    return (rewards - reward_mean) / jnp.sqrt(reward_var + 1e-05)


def gathered_plan(
    prompts, gate_weight, up_weight, reward_head, member_seeds, counters, member_ranks
):
    members_here, seq_len, width = prompts.shape
    own_rows, own_cols = gate_weight.shape
    pop_index = lax.axis_index("pop")
    column_ids = lax.axis_index("mp") * own_cols + jnp.arange(own_cols, dtype=jnp.int32)
    small = lax.all_gather(
        jnp.stack([member_seeds, counters, member_ranks]), "pop", axis=1, tiled=True
    )
    new_gate, new_up = fresh_weights(
        gate_weight, up_weight, small[0], small[1], small[2], pop_index * own_rows, column_ids
    )
    flat_rows = prompts.reshape(members_here * seq_len, width)
    later = counters + 1
    positions = jnp.arange(width, dtype=jnp.int32)

    def projected(weight, slot):
        base = jnp.dot(
            flat_rows,
            lax.all_gather(weight, "pop", axis=0, tiled=True),
            preferred_element_type=jnp.float32,
        ).reshape(members_here, seq_len, own_cols)
        vector = factor_rows(member_seeds, later, slot, positions).astype(jnp.bfloat16)
        column = factor_rows(member_seeds, later, slot + 1, column_ids)
        proj = jnp.einsum("mld,md->ml", prompts, vector, preferred_element_type=jnp.float32)
        return base + sigma_perturb * proj[:, :, None] * column[:, None, :]

    hidden = (jax.nn.silu(projected(new_gate, 0)) * projected(new_up, 2)).astype(jnp.bfloat16)
    partial = jnp.einsum("mlf,f->m", hidden, reward_head, preferred_element_type=jnp.float32)
    rewards = lax.all_gather(lax.psum(partial, "mp"), "pop", axis=0, tiled=True) / seq_len
    own = lax.dynamic_slice_in_dim(normalized(rewards), pop_index * members_here, members_here)
    return new_gate, new_up, own


def partial_kernel(count, index_ref, *refs):
    x_refs, w_refs, out_ref = refs[:count], refs[count : 2 * count], refs[2 * count]
    columns = w_refs[0].shape[2]
    rows = jnp.concatenate([r[...] for r in x_refs], axis=1)
    for part in range(2):
        weights = jnp.concatenate([w[part] for w in w_refs], axis=0)
        out_ref[:, part * columns : (part + 1) * columns] = jnp.dot(
            rows, weights, preferred_element_type=jnp.float32
        )


def partial_product(rows, index, chunks):
    count = len(chunks)
    tokens = rows.shape[0]
    _, depth, columns = chunks[0].shape
    tile = min(512, tokens)
    return pl.pallas_call(
        lambda *refs: partial_kernel(count, *refs),
        out_shape=jax.ShapeDtypeStruct((tokens, 2 * columns), jnp.float32),
        grid_spec=pltpu.PrefetchScalarGridSpec(
            num_scalar_prefetch=1,
            grid=(tokens // tile,),
            in_specs=[
                pl.BlockSpec((tile, depth), lambda i, idx, k=k: (i, idx[k])) for k in range(count)
            ]
            + [pl.BlockSpec((2, depth, columns), lambda i, idx: (0, 0, 0))] * count,
            out_specs=pl.BlockSpec((tile, 2 * columns), lambda i, idx: (i, 0)),
        ),
        compiler_params=pltpu.CompilerParams(vmem_limit_bytes=48 * 1024 * 1024),
        cost_estimate=pl.CostEstimate(
            flops=4 * tokens * depth * count * columns,
            bytes_accessed=2 * tokens * depth * count + 8 * tokens * columns + 4 * count * depth * columns,
            transcendentals=0,
        ),
    )(index, *([rows] * count), *chunks)


def final_kernel(count, seq, index_ref, *refs):
    x_refs, w_refs = refs[:count], refs[count : 2 * count]
    base_ref, proj_ref, col_ref, head_ref, out_ref = refs[2 * count :]
    columns = w_refs[0].shape[2]
    rows = jnp.concatenate([r[...] for r in x_refs], axis=1)
    values = []
    for part in range(2):
        weights = jnp.concatenate([w[part] for w in w_refs], axis=0)
        value = base_ref[:, part * columns : (part + 1) * columns] + jnp.dot(
            rows, weights, preferred_element_type=jnp.float32
        )
        members = []
        for i in range(rows.shape[0] // seq):
            members.append(
                value[i * seq : (i + 1) * seq]
                + sigma_perturb
                * proj_ref[i * seq : (i + 1) * seq, part : part + 1]
                * col_ref[0, part, i : i + 1, :]
            )
        values.append(members)
    for i, (gate, up) in enumerate(zip(*values)):
        hidden = (gate / (1.0 + jnp.exp(-gate)) * up).astype(jnp.bfloat16)
        terms = hidden.astype(jnp.float32) * head_ref[...].astype(jnp.float32)
        out_ref[i] = jnp.sum(terms.reshape(seq // 8, 8, columns), axis=0)


def final_rewards(rows, index, chunks, base, proj, cols, head, seq):
    count = len(chunks)
    tokens = rows.shape[0]
    _, depth, columns = chunks[0].shape
    group = cols.shape[2]
    tile = group * seq
    return pl.pallas_call(
        lambda *refs: final_kernel(count, seq, *refs),
        out_shape=jax.ShapeDtypeStruct((tokens // seq, 8, columns), jnp.float32),
        grid_spec=pltpu.PrefetchScalarGridSpec(
            num_scalar_prefetch=1,
            grid=(tokens // tile,),
            in_specs=[
                pl.BlockSpec((tile, depth), lambda i, idx, k=k: (i, idx[k])) for k in range(count)
            ]
            + [pl.BlockSpec((2, depth, columns), lambda i, idx: (0, 0, 0))] * count
            + [
                pl.BlockSpec((tile, 2 * columns), lambda i, idx: (i, 0)),
                pl.BlockSpec((tile, 2), lambda i, idx: (i, 0)),
                pl.BlockSpec((1, 2, group, columns), lambda i, idx: (i, 0, 0, 0)),
                pl.BlockSpec((1, columns), lambda i, idx: (0, 0)),
            ],
            out_specs=pl.BlockSpec((group, 8, columns), lambda i, idx: (i, 0, 0)),
        ),
        compiler_params=pltpu.CompilerParams(vmem_limit_bytes=48 * 1024 * 1024),
        cost_estimate=pl.CostEstimate(
            flops=4 * tokens * depth * count * columns,
            bytes_accessed=2 * tokens * depth * count + 8 * tokens * columns + 4 * count * depth * columns,
            transcendentals=tokens * columns,
        ),
    )(index, *([rows] * count), *chunks, base, proj, cols, head)


def tree_sum(terms):
    while len(terms) > 1:
        half = len(terms) // 2
        terms = [terms[i] + terms[i + half] for i in range(half)]
    return terms[0]


def spread_plan(planes, prompts, gate_weight, up_weight, reward_head, member_seeds, counters, member_ranks):
    members_here, seq, width = prompts.shape
    own_rows, own_cols = gate_weight.shape
    n_mp = members_here
    pop_index = lax.axis_index("pop")
    mp_index = lax.axis_index("mp")
    z, core = pop_index // CORES, pop_index % CORES
    block = own_cols // planes

    def pairs(move, keep=lambda z: True):
        out = []
        for a in range(planes):
            for c in range(CORES):
                for m in range(n_mp):
                    target = move(a, c, m)
                    if keep(a) and 0 <= target[0] < planes:
                        source = (a * CORES + c) * n_mp + m
                        out.append((source, (target[0] * CORES + target[1]) * n_mp + target[2]))
        return out

    def send(value, move, keep=lambda z: True):
        return lax.ppermute(value, AXES, pairs(move, keep))

    def swap_core(value):
        return send(value, lambda a, c, m: (a, 1 - c, m))

    def swap_in_plane(value, bit):
        return send(value, lambda a, c, m: (a, c, m ^ bit))

    def turn(value, s):
        return send(value, lambda a, c, m: ((a + s) % planes, c, m))

    own_member = lax.dynamic_index_in_dim(prompts, mp_index, 0, keepdims=False)
    up_hops, down_hops = [own_member], [own_member]
    for s in range(1, planes):
        up_hops.append(send(up_hops[-1], lambda a, c, m: (a + 1, c, m), lambda a: a >= s - 1))
        down_hops.append(
            send(down_hops[-1], lambda a, c, m: (a - 1, c, m), lambda a: a <= planes - s)
        )

    small = jnp.stack([member_seeds, counters, member_ranks])
    small_here = jnp.stack([small] + [turn(small, s) for s in range(1, planes)])
    small_other = swap_core(small_here)
    every = jnp.concatenate([small_here, small_other]).transpose(1, 0, 2).reshape(3, -1)

    arrivals = []
    for a in range(planes):
        order = []
        for s in range(1, planes):
            if a - s >= 0:
                order.append((0, s, a - s))
            if a + s < planes:
                order.append((1, s, a + s))
        arrivals.append(order)

    groups = [prompts.reshape(members_here * seq, width)]
    group_seeds = [(member_seeds, counters)]
    group_ids = [pop_index * members_here + jnp.arange(members_here, dtype=jnp.int32)]
    half = seq // 2
    for r in range(planes - 1):
        picks = {}
        for a in range(planes):
            picks.setdefault(arrivals[a][r][:2], []).append(a)
        block_here = None
        for (way, s), where in picks.items():
            value = (up_hops, down_hops)[way][s]
            if block_here is None:
                block_here = value
            else:
                here = (z == where[0])
                for a in where[1:]:
                    here = here | (z == a)
                block_here = jnp.where(here, value, block_here)
        across_x = swap_in_plane(block_here, 1)
        across_y = swap_in_plane(block_here, 2)
        corner_top = swap_in_plane(across_y[:half], 1)
        corner_low = swap_in_plane(across_x[half:], 2)
        groups.append(
            jnp.concatenate([block_here, across_x, across_y, corner_top, corner_low], axis=0)
        )
        source = jnp.int32(0)
        for a in range(planes):
            source = jnp.where(z == a, arrivals[a][r][2], source)
        back = (z - source) % planes
        rel = mp_index ^ jnp.arange(members_here, dtype=jnp.int32)
        chosen = jnp.int32(0)
        for s in range(1, planes):
            chosen = jnp.where(back == s, small_here[s], chosen)
        order = (rel[:, None] == jnp.arange(members_here, dtype=jnp.int32)[None, :]).astype(jnp.int32)
        picked = jnp.sum(order[None] * chosen[:, None, :], axis=2)
        group_seeds.append((picked[0], picked[1]))
        group_ids.append((source * CORES + core) * members_here + rel)

    column_ids = mp_index * own_cols + jnp.arange(own_cols, dtype=jnp.int32)
    new_gate, new_up = fresh_weights(
        gate_weight, up_weight, every[0], every[1], every[2], pop_index * own_rows, column_ids
    )

    def for_plane(target):
        start = target * block
        return jnp.stack(
            [
                lax.dynamic_slice_in_dim(new_gate, start, block, axis=1),
                lax.dynamic_slice_in_dim(new_up, start, block, axis=1),
            ]
        )

    order_of = [0] + sorted(range(1, planes), key=lambda s: (-min(s, planes - s), s))
    chunks, places = [], []
    for s in order_of:
        mine = for_plane((z + s) % planes)
        if s:
            mine = turn(mine, s)
        chunks.append((mine, swap_core(mine)))
        source = (z - s) % planes
        places.append((source * CORES + core, source * CORES + 1 - core))

    my_columns = mp_index * own_cols + z * block + jnp.arange(block, dtype=jnp.int32)
    positions = jnp.arange(width, dtype=jnp.int32)
    projs, cols = [], []
    for rows, (seeds, counts) in zip(groups, group_seeds):
        both_p, both_c = [], []
        for slot in (0, 2):
            vector = factor_rows(seeds, counts + 1, slot, positions).astype(jnp.bfloat16)
            both_c.append(factor_rows(seeds, counts + 1, slot + 1, my_columns))
            both_p.append(
                jnp.einsum(
                    "mld,md->ml",
                    rows.reshape(members_here, seq, width),
                    vector,
                    preferred_element_type=jnp.float32,
                ).reshape(-1)
            )
        projs.append(jnp.stack(both_p, axis=1))
        cols.append(jnp.stack(both_c))

    early = [c for pair in chunks[:-1] for c in pair]
    early_index = jnp.stack([p for pair in places[:-1] for p in pair])
    head = lax.dynamic_slice_in_dim(reward_head, z * block, block).reshape(1, block)
    sums = []
    for rows, proj, col in zip(groups, projs, cols):
        base = partial_product(rows, early_index, early)
        out = final_rewards(
            rows, jnp.stack(places[-1]), list(chunks[-1]), base, proj, col[None], head, seq
        )
        sums.append(out)
    sums = jnp.concatenate(sums).reshape(planes * members_here, -1).sum(axis=1)

    ids = jnp.concatenate(group_ids)
    total = planes * CORES * members_here
    rewards = jnp.sum(
        jnp.where(ids[:, None] == jnp.arange(total, dtype=jnp.int32)[None, :], sums[:, None], 0.0),
        axis=0,
    ).reshape(1, total)
    rewards = (rewards + swap_in_plane(rewards, 1)) + (
        swap_in_plane(rewards, 2) + swap_in_plane(rewards, 3)
    )
    rewards = tree_sum([rewards] + [turn(rewards, s) for s in range(1, planes)])
    rewards = (rewards + swap_core(rewards)).reshape(total) / seq
    own = lax.dynamic_slice_in_dim(normalized(rewards), pop_index * members_here, members_here)
    return new_gate, new_up, own


def solution(mesh):
    n_pop, n_mp = mesh.shape["pop"], mesh.shape["mp"]
    planes = n_pop // CORES

    def shards(prompts, gate_weight, *rest):
        members_here, seq, width = prompts.shape
        own_cols = gate_weight.shape[1]
        gathered = 2 * width * own_cols + members_here * seq * width
        spread = 2 * width * own_cols // planes + planes * members_here * seq * width
        square = n_mp == 4 and members_here == n_mp and planes & (planes - 1) == 0
        if square and own_cols % (128 * planes) == 0 and spread < gathered:
            return spread_plan(planes, prompts, gate_weight, *rest)
        return gathered_plan(prompts, gate_weight, *rest)

    in_specs = (
        P("pop", None, None),
        P("pop", "mp"),
        P("pop", "mp"),
        P("mp"),
        P("pop"),
        P("pop"),
        P("pop"),
    )
    out_specs = (P("pop", "mp"), P("pop", "mp"), P("pop"))
    return jax.shard_map(shards, mesh=mesh, in_specs=in_specs, out_specs=out_specs, check_vma=False)
```

```python
import jax
import jax.numpy as jnp
from jax import lax
from jax.experimental import pallas as pl
from jax.experimental.pallas import tpu as pltpu
from jax.sharding import PartitionSpec as P

sigma_perturb = 0.004
learn_rate = 0.0016
AXES = ("pop", "mp")
CORES = 2


def shift_down(number, amount):
    return lax.shift_right_logical(number, jnp.full_like(number, amount))


def mix_bits(number):
    number = number ^ shift_down(number, 16)
    number = number * 2146121005
    number = number ^ shift_down(number, 15)
    number = number * -2073254261
    return number ^ shift_down(number, 16)


def factor_rows(seed_list, counter_list, slot, positions):
    anchor = mix_bits(
        seed_list * 1103515245 + mix_bits(counter_list * 668265263 + slot * 374761393)
    )
    hashed = mix_bits(anchor[:, None] + positions[None, :] * -1640531535)
    uniform_part = shift_down(hashed, 8).astype(jnp.float32) * (1.0 / 16777216.0)
    return (2.0 * uniform_part - 1.0 + 1.0 / 16777216.0) * 1.7320508075688772


def fresh_weights(gate_weight, up_weight, seeds, counters, ranks, row_start, column_ids):
    members_all = seeds.shape[0]
    fitness = (ranks.astype(jnp.float32) + 0.5) / members_all - 0.5
    scaling = learn_rate / (members_all * sigma_perturb)
    row_ids = row_start + jnp.arange(gate_weight.shape[0], dtype=jnp.int32)

    def fresh(weight, slot):
        right = factor_rows(seeds, counters, slot + 1, column_ids).astype(jnp.bfloat16)
        left = (factor_rows(seeds, counters, slot, row_ids) * fitness[:, None]).astype(jnp.bfloat16)
        update = scaling * jnp.dot(left.T, right, preferred_element_type=jnp.float32)
        return (weight.astype(jnp.float32) + update).astype(jnp.bfloat16)

    return fresh(gate_weight, 0), fresh(up_weight, 2)


def normalized(rewards):
    reward_mean = jnp.mean(rewards)
    reward_var = jnp.mean((rewards - reward_mean) ** 2)
    return (rewards - reward_mean) / jnp.sqrt(reward_var + 1e-05)


def gathered_plan(
    prompts, gate_weight, up_weight, reward_head, member_seeds, counters, member_ranks
):
    members_here, seq_len, width = prompts.shape
    own_rows, own_cols = gate_weight.shape
    pop_index = lax.axis_index("pop")
    column_ids = lax.axis_index("mp") * own_cols + jnp.arange(own_cols, dtype=jnp.int32)
    small = lax.all_gather(
        jnp.stack([member_seeds, counters, member_ranks]), "pop", axis=1, tiled=True
    )
    new_gate, new_up = fresh_weights(
        gate_weight, up_weight, small[0], small[1], small[2], pop_index * own_rows, column_ids
    )
    flat_rows = prompts.reshape(members_here * seq_len, width)
    later = counters + 1
    positions = jnp.arange(width, dtype=jnp.int32)

    def projected(weight, slot):
        base = jnp.dot(
            flat_rows,
            lax.all_gather(weight, "pop", axis=0, tiled=True),
            preferred_element_type=jnp.float32,
        ).reshape(members_here, seq_len, own_cols)
        vector = factor_rows(member_seeds, later, slot, positions).astype(jnp.bfloat16)
        column = factor_rows(member_seeds, later, slot + 1, column_ids)
        proj = jnp.einsum("mld,md->ml", prompts, vector, preferred_element_type=jnp.float32)
        return base + sigma_perturb * proj[:, :, None] * column[:, None, :]

    hidden = (jax.nn.silu(projected(new_gate, 0)) * projected(new_up, 2)).astype(jnp.bfloat16)
    partial = jnp.einsum("mlf,f->m", hidden, reward_head, preferred_element_type=jnp.float32)
    rewards = lax.all_gather(lax.psum(partial, "mp"), "pop", axis=0, tiled=True) / seq_len
    own = lax.dynamic_slice_in_dim(normalized(rewards), pop_index * members_here, members_here)
    return new_gate, new_up, own


def product_kernel(plan, counts, finish, starts_ref, *refs):
    refs = list(refs)
    x_refs, w_refs, base_refs = [[refs.pop(0) for _ in range(count)] for count in counts]
    if finish:
        proj_ref, col_ref, head_ref = [refs.pop(0) for _ in range(3)]
        head = head_ref[...].astype(jnp.float32)
    out_ref = refs.pop(0)
    columns = w_refs[0].shape[2]
    for i, (segments, first_chunk, base) in enumerate(plan):
        values = [None, None]
        for k in range(first_chunk, len(w_refs)):
            depth = w_refs[k].shape[1]
            at = pl.ds(pl.multiple_of(starts_ref[k], depth), depth)
            rows = [x_refs[x][pl.ds(first, count), at] for x, first, count in segments]
            rows = rows[0] if len(rows) == 1 else jnp.concatenate(rows)
            for part in range(2):
                term = jnp.dot(rows, w_refs[k][part], preferred_element_type=jnp.float32)
                values[part] = term if values[part] is None else values[part] + term
        seq = values[0].shape[0]
        for part in range(2):
            if base is not None:
                at = pl.ds(base[1], seq)
                values[part] += base_refs[base[0]][at, part * columns : (part + 1) * columns]
            if not finish:
                out_ref[i * seq : (i + 1) * seq, part * columns : (part + 1) * columns] = values[part]
        if finish:
            gate, up = [
                values[part]
                + sigma_perturb
                * proj_ref[i * seq : (i + 1) * seq, part : part + 1]
                * col_ref[part, i : i + 1, :]
                for part in range(2)
            ]
            hidden = (gate / (1.0 + jnp.exp(-gate)) * up).astype(jnp.bfloat16)
            terms = hidden.astype(jnp.float32) * head
            out_ref[i] = jnp.sum(terms.reshape(seq // 8, 8, columns), axis=0)


def product(members, chunks, finish=None):
    depths = [chunk.shape[1] for _, chunk in chunks]
    columns = chunks[0][1].shape[2]
    arrays, base_arrays, plan = [], [], []

    def number(array, known):
        for i, other in enumerate(known):
            if other is array:
                return i
        known.append(array)
        return len(known) - 1

    for segments, first_chunk, base in members:
        placed = [(number(a, arrays), first, rows) for a, first, rows in segments]
        plan.append((placed, first_chunk, base and (number(base[0], base_arrays), base[1])))
    seq = sum(rows for _, _, rows in members[0][0])
    total = seq * len(members)
    work = sum(seq * sum(depths[first:]) for _, first, _ in members)
    vmem = pl.BlockSpec(memory_space=pltpu.VMEM)
    operands = [
        *arrays,
        *[chunk for _, chunk in chunks],
        *base_arrays,
        *(finish or ()),
    ]
    shape = (len(members), 8, columns) if finish else (total, 2 * columns)
    held = sum(a.size * a.dtype.itemsize for a in operands) + 4 * total * 2 * columns
    counts = [len(arrays), len(chunks), len(base_arrays)]
    return pl.pallas_call(
        lambda *refs: product_kernel(plan, counts, finish, *refs),
        out_shape=jax.ShapeDtypeStruct(shape, jnp.float32),
        in_specs=[pl.BlockSpec(memory_space=pltpu.SMEM)] + [vmem] * len(operands),
        out_specs=vmem,
        compiler_params=pltpu.CompilerParams(vmem_limit_bytes=held + 4 * 1024 * 1024),
        cost_estimate=pl.CostEstimate(
            flops=4 * work * columns,
            bytes_accessed=2 * work + 16 * total * columns + 4 * sum(depths) * columns,
            transcendentals=total * columns if finish else 0,
        ),
    )(jnp.stack([start for start, _ in chunks]), *operands)


def tree_sum(terms):
    while len(terms) > 1:
        half = len(terms) // 2
        terms = [terms[i] + terms[i + half] for i in range(half)]
    return terms[0]


def spread_plan(planes, prompts, gate_weight, up_weight, reward_head, member_seeds, counters, member_ranks):
    members_here, seq, width = prompts.shape
    own_rows, own_cols = gate_weight.shape
    n_mp = members_here
    pop_index = lax.axis_index("pop")
    mp_index = lax.axis_index("mp")
    z, core = pop_index // CORES, pop_index % CORES
    block = own_cols // planes

    def pairs(move, keep=lambda z: True):
        out = []
        for a in range(planes):
            for c in range(CORES):
                for m in range(n_mp):
                    target = move(a, c, m)
                    if keep(a) and 0 <= target[0] < planes:
                        source = (a * CORES + c) * n_mp + m
                        out.append((source, (target[0] * CORES + target[1]) * n_mp + target[2]))
        return out

    def send(value, move, keep=lambda z: True):
        return lax.ppermute(value, AXES, pairs(move, keep))

    def swap_core(value):
        return send(value, lambda a, c, m: (a, 1 - c, m))

    def swap_in_plane(value, bit):
        return send(value, lambda a, c, m: (a, c, m ^ bit))

    def turn(value, s):
        return send(value, lambda a, c, m: ((a + s) % planes, c, m))

    def tie(*values):
        return lax.optimization_barrier(values)

    def up(value, s):
        return send(value, lambda a, c, m: (a + 1, c, m), lambda a: a >= s - 1)

    def down(value, s):
        return send(value, lambda a, c, m: (a - 1, c, m), lambda a: a <= planes - s)

    arrivals = []
    for a in range(planes):
        order = []
        for s in range(1, planes):
            if a - s >= 0:
                order.append((0, s, a - s))
            if a + s < planes:
                order.append((1, s, a + s))
        arrivals.append(order)

    def by_plane(numbers):
        value = jnp.int32(numbers[0])
        for a in range(1, planes):
            value = jnp.where(z == a, numbers[a], value)
        return value

    def round_block(r):
        picks = {}
        for a in range(planes):
            picks.setdefault(arrivals[a][r - 1][:2], []).append(a)
        chosen = None
        for (way, s), where in picks.items():
            here = z == where[0]
            for a in where[1:]:
                here = here | (z == a)
            value = hops[way][s]
            chosen = value if chosen is None else jnp.where(here, value, chosen)
        return chosen

    def piece(weights, s, first, count):
        corner = (first, (z + s) % planes * block)
        return jnp.stack([lax.dynamic_slice(w, corner, (count, block)) for w in weights])

    small = jnp.stack([member_seeds, counters, member_ranks])
    own_member = lax.dynamic_index_in_dim(prompts, mp_index, 0, keepdims=False)
    hops = [[own_member, up(own_member, 1)], [own_member, down(own_member, 1)]]
    small_here = jnp.stack([small] + [turn(small, s) for s in range(1, planes)])
    small_other = swap_core(small_here)
    every = jnp.concatenate([small_here, small_other]).transpose(1, 0, 2).reshape(3, -1)
    head = lax.dynamic_slice_in_dim(reward_head, z * block, block).reshape(1, block)
    my_columns = mp_index * own_cols + z * block + jnp.arange(block, dtype=jnp.int32)
    positions = jnp.arange(width, dtype=jnp.int32)
    lanes = jnp.arange(members_here, dtype=jnp.int32)

    rel = mp_index ^ lanes
    rel_hot = (rel[:, None] == lanes[None, :]).astype(jnp.int32)
    flat = prompts.reshape(members_here * seq, width)
    members = [[(flat, i * seq, seq)] for i in range(members_here)]
    group_ids = [pop_index * members_here + lanes]
    picked = [(member_seeds, counters)]
    for r in range(1, planes):
        source = by_plane([arrivals[a][r - 1][2] for a in range(planes)])
        back = (z - source) % planes
        chosen = jnp.int32(0)
        for s in range(1, planes):
            chosen = jnp.where(back == s, small_here[s], chosen)
        chosen = jnp.sum(rel_hot[None] * chosen[:, None, :], axis=2)
        picked.append((chosen[0], chosen[1]))
        group_ids.append((source * CORES + core) * members_here + rel)

    def perturbed(r):
        seeds, counts = picked[r]
        vectors = jnp.stack(
            [factor_rows(seeds, counts + 1, slot, positions).astype(jnp.bfloat16) for slot in (0, 2)],
            axis=1,
        )
        found = [
            lax.dot_general(
                array[first : first + rows],
                vectors[i],
                (((1,), (1,)), ((), ())),
                preferred_element_type=jnp.float32,
            )
            for i in range(members_here)
            for array, first, rows in members[r * members_here + i]
        ]
        columns = [factor_rows(seeds, counts + 1, slot + 1, my_columns) for slot in (0, 2)]
        return jnp.concatenate(found), jnp.stack(columns)

    projs, cols = map(lambda v: [v], perturbed(0))

    column_ids = mp_index * own_cols + jnp.arange(own_cols, dtype=jnp.int32)
    weights = fresh_weights(
        gate_weight, up_weight, every[0], every[1], every[2], pop_index * own_rows, column_ids
    )
    new_gate, new_up = weights
    far_first = sorted(range(1, planes), key=lambda s: (-min(s, planes - s), s))
    half_rows = own_rows // 2
    queue = [(s, 0, own_rows) for s in far_first[:-1]]
    queue += [(far_first[-1], first, half_rows) for first in (0, half_rows)]
    leave = {planes - 2: queue[:1], planes - 1: queue[1:-1], planes: queue[-1:]}
    outgoing = {key: piece(weights, *key) for key in queue}
    landed = {(0, 0, own_rows): piece(weights, 0, 0, own_rows)}
    chunks = []

    def add_chunks(key):
        s, first, _ = key
        plane = (z - s) % planes * CORES
        return [
            ((plane + core) * own_rows + first, landed[key]),
            ((plane + 1 - core) * own_rows + first, swap_core(landed[key])),
        ]

    half = seq // 2
    fresh = [(0, 0, own_rows)]
    across_x = across_y = corner_x = corner_y = None
    bases, held_back, early = [], 0, 0

    def on(some, first_chunk, base=None):
        return [
            (m, first_chunk, base if base is None else (base, i * seq)) for i, m in enumerate(some)
        ]

    hops[0][1], hops[1][1] = tie(hops[0][1], hops[1][1])
    for phase in range(1, planes + 1):
        if phase < planes - 1:
            hops[0].append(up(hops[0][phase], phase + 1))
            hops[1].append(down(hops[1][phase], phase + 1))
        to_x, to_y = [], []
        if phase < planes:
            here = round_block(phase)
            to_x.append(here)
            to_y.append(here)
        if phase > 1:
            to_x.append(across_y[:half])
            to_y.append(across_x[half:seq])
        new_x = swap_in_plane(jnp.concatenate(to_x), 1)
        new_y = swap_in_plane(jnp.concatenate(to_y), 2)
        for key in leave.get(phase, ()):
            landed[key] = turn(outgoing[key], key[0])
        new_chunks = [c for key in fresh for c in add_chunks(key)]
        fresh = leave.get(phase, ())
        known = chunks + new_chunks
        if phase == planes - 1:
            early = len(members)
            bases = [product(on(members, 0), known)]
            held_back = len(known)
        elif phase == planes:
            bases.append(product(on(members[:early], 0, bases[0]), known[held_back:]))
            bases.append(product(on(members[early:], 0), known))
        parts = (hops, new_x, new_y, landed, new_chunks, outgoing, bases)
        hops, new_x, new_y, landed, new_chunks, outgoing, bases = tie(*parts)
        chunks += new_chunks
        if phase > 1:
            first = seq if phase < planes else 0
            members.append([(new_x, first, half), (new_y, first, half)])
            proj, col = perturbed(phase - 1)
            projs.append(proj)
            cols.append(col)
        if phase < planes:
            members += [[(here, 0, seq)], [(new_x, 0, seq)], [(new_y, 0, seq)]]
        across_x, across_y = new_x, new_y

    last = [c for key in fresh for c in add_chunks(key)]
    plan = on(members[:early], len(chunks), bases[1])
    plan += on(members[early:-1], len(chunks), bases[2]) + on(members[-1:], 0)
    finish = (jnp.concatenate(projs), jnp.concatenate(cols, axis=1), head)
    sums = product(plan, chunks + last, finish).reshape(len(members), -1).sum(axis=1)

    ids = jnp.concatenate(group_ids)
    total = planes * CORES * members_here
    rewards = jnp.sum(
        jnp.where(ids[:, None] == jnp.arange(total, dtype=jnp.int32)[None, :], sums[:, None], 0.0),
        axis=0,
    ).reshape(1, total)
    rewards = (rewards + swap_in_plane(rewards, 1)) + (
        swap_in_plane(rewards, 2) + swap_in_plane(rewards, 3)
    )
    rewards = tree_sum([rewards] + [turn(rewards, s) for s in range(1, planes)])
    rewards = (rewards + swap_core(rewards)).reshape(total) / seq
    own = lax.dynamic_slice_in_dim(normalized(rewards), pop_index * members_here, members_here)
    return new_gate, new_up, own


def solution(mesh):
    n_pop, n_mp = mesh.shape["pop"], mesh.shape["mp"]
    planes = n_pop // CORES

    def shards(prompts, gate_weight, *rest):
        members_here, seq, width = prompts.shape
        own_cols = gate_weight.shape[1]
        gathered = 2 * width * own_cols + members_here * seq * width
        spread = 2 * width * own_cols // planes + planes * members_here * seq * width
        square = n_mp == 4 and members_here == n_mp and planes & (planes - 1) == 0
        if square and own_cols % (128 * planes) == 0 and spread < gathered:
            return spread_plan(planes, prompts, gate_weight, *rest)
        return gathered_plan(prompts, gate_weight, *rest)

    in_specs = (
        P("pop", None, None),
        P("pop", "mp"),
        P("pop", "mp"),
        P("mp"),
        P("pop"),
        P("pop"),
        P("pop"),
    )
    out_specs = (P("pop", "mp"), P("pop", "mp"), P("pop"))
    return jax.shard_map(shards, mesh=mesh, in_specs=in_specs, out_specs=out_specs, check_vma=False)
```

```python
import math

import jax
import jax.numpy as jnp
from jax import lax
from jax.experimental import pallas as pl
from jax.experimental.pallas import tpu as pltpu
from jax.sharding import PartitionSpec as P

sigma_perturb = 0.004
learn_rate = 0.0016
AXES = ("pop", "mp")
CORES = 2
SPARE_BYTES = 4 * 1024 * 1024


def shift_down(number, amount):
    return lax.shift_right_logical(number, jnp.full_like(number, amount))


def mix_bits(number):
    number = number ^ shift_down(number, 16)
    number = number * 2146121005
    number = number ^ shift_down(number, 15)
    number = number * -2073254261
    return number ^ shift_down(number, 16)


def factor_rows(seed_list, counter_list, slot, positions):
    anchor = mix_bits(
        seed_list * 1103515245 + mix_bits(counter_list * 668265263 + slot * 374761393)
    )
    hashed = mix_bits(anchor[:, None] + positions[None, :] * -1640531535)
    uniform_part = shift_down(hashed, 8).astype(jnp.float32) * (1.0 / 16777216.0)
    return (2.0 * uniform_part - 1.0 + 1.0 / 16777216.0) * 1.7320508075688772


def fresh_weights(gate_weight, up_weight, seeds, counters, ranks, row_start, column_ids):
    members_all = seeds.shape[0]
    fitness = (ranks.astype(jnp.float32) + 0.5) / members_all - 0.5
    scaling = learn_rate / (members_all * sigma_perturb)
    row_ids = row_start + jnp.arange(gate_weight.shape[0], dtype=jnp.int32)

    def fresh(weight, slot):
        right = factor_rows(seeds, counters, slot + 1, column_ids).astype(jnp.bfloat16)
        left = (factor_rows(seeds, counters, slot, row_ids) * fitness[:, None]).astype(jnp.bfloat16)
        update = scaling * jnp.dot(left.T, right, preferred_element_type=jnp.float32)
        return (weight.astype(jnp.float32) + update).astype(jnp.bfloat16)

    return fresh(gate_weight, 0), fresh(up_weight, 2)


def normalized(rewards):
    reward_mean = jnp.mean(rewards)
    reward_var = jnp.mean((rewards - reward_mean) ** 2)
    return (rewards - reward_mean) / jnp.sqrt(reward_var + 1e-05)


def gathered_plan(
    prompts, gate_weight, up_weight, reward_head, member_seeds, counters, member_ranks
):
    members_here, seq_len, width = prompts.shape
    own_rows, own_cols = gate_weight.shape
    pop_index = lax.axis_index("pop")
    column_ids = lax.axis_index("mp") * own_cols + jnp.arange(own_cols, dtype=jnp.int32)
    small = lax.all_gather(
        jnp.stack([member_seeds, counters, member_ranks]), "pop", axis=1, tiled=True
    )
    new_gate, new_up = fresh_weights(
        gate_weight, up_weight, small[0], small[1], small[2], pop_index * own_rows, column_ids
    )
    flat_rows = prompts.reshape(members_here * seq_len, width)
    later = counters + 1
    positions = jnp.arange(width, dtype=jnp.int32)

    def projected(weight, slot):
        base = jnp.dot(
            flat_rows,
            lax.all_gather(weight, "pop", axis=0, tiled=True),
            preferred_element_type=jnp.float32,
        ).reshape(members_here, seq_len, own_cols)
        vector = factor_rows(member_seeds, later, slot, positions).astype(jnp.bfloat16)
        column = factor_rows(member_seeds, later, slot + 1, column_ids)
        proj = jnp.einsum("mld,md->ml", prompts, vector, preferred_element_type=jnp.float32)
        return base + sigma_perturb * proj[:, :, None] * column[:, None, :]

    hidden = (jax.nn.silu(projected(new_gate, 0)) * projected(new_up, 2)).astype(jnp.bfloat16)
    partial = jnp.einsum("mlf,f->m", hidden, reward_head, preferred_element_type=jnp.float32)
    rewards = lax.all_gather(lax.psum(partial, "mp"), "pop", axis=0, tiled=True) / seq_len
    own = lax.dynamic_slice_in_dim(normalized(rewards), pop_index * members_here, members_here)
    return new_gate, new_up, own


def product_kernel(plan, counts, plane_of, seq, ranked, vectored, read_out, starts_ref, *refs):
    refs = list(refs)
    x_refs, w_refs, base_refs = [[refs.pop(0) for _ in range(count)] for count in counts]
    if ranked:
        proj_ref, col_ref = refs.pop(0), refs.pop(0)
    if vectored:
        vector_ref, vector_col_ref = refs.pop(0), refs.pop(0)
    if read_out:
        head_ref = refs.pop(0)
        head = head_ref[...].astype(jnp.float32)
    out_ref, weights = refs.pop(0), refs.pop(0)
    rows, totals = [], []
    for _, _, base, _ in plan:
        rows.append(refs.pop(0))
        totals.append(refs.pop(0) if base is not None or not read_out else None)
    row_sems, weight_sems, total_sems = refs
    columns = weights.shape[2]
    n_planes = 1 + plane_of[-1]
    plane_rows = weights.shape[1] // n_planes
    weight_copies = []
    for k, w_ref in enumerate(w_refs):
        depth = w_ref.shape[1]
        at = plane_of[k] * plane_rows + pl.multiple_of(starts_ref[len(w_refs) + k], depth)
        weight_copies.append(pltpu.make_async_copy(w_ref, weights.at[:, pl.ds(at, depth)], weight_sems.at[k]))
    group_copies = []
    for g, (segments, first, base, _) in enumerate(plan):
        copies = []
        row = 0
        for i, (x, start_row, count) in enumerate(segments):
            for plane in range(first, n_planes):
                start = pl.multiple_of(starts_ref[plane_of.index(plane)], plane_rows)
                copies.append(
                    pltpu.make_async_copy(
                        x_refs[x].at[pl.ds(start_row, count), pl.ds(start, plane_rows)],
                        rows[g].at[pl.ds(row, count), pl.ds((plane - first) * plane_rows, plane_rows)],
                        row_sems.at[g, i, plane],
                    )
                )
            row += count
        if base is not None:
            source = base_refs[base[0]].at[pl.ds(base[1], row)]
            copies.append(pltpu.make_async_copy(source, totals[g], total_sems.at[g]))
        group_copies.append(copies)
    started = set()
    for g, (_, first, _, _) in enumerate(plan):
        for k, copy in enumerate(weight_copies):
            if plane_of[k] >= first and k not in started:
                started.add(k)
                copy.start()
        for copy in group_copies[g]:
            copy.start()
    done_rows, out_copies = 0, []
    for g, (_, first, base, own_vectors) in enumerate(plan):
        for k in sorted(started):
            if plane_of[k] >= first:
                started.remove(k)
                weight_copies[k].wait()
        for copy in group_copies[g]:
            copy.wait()
        count = rows[g].shape[0]
        values = [
            jnp.dot(rows[g][...], weights[part, first * plane_rows :], preferred_element_type=jnp.float32)
            for part in range(2)
        ]
        for i in range(count // seq):
            here = slice(i * seq, (i + 1) * seq)
            there = slice(done_rows + i * seq, done_rows + (i + 1) * seq)
            member = done_rows // seq + i
            found = []
            vector = None
            for plane in range(first, n_planes if own_vectors is not None else first):
                start = pl.multiple_of(starts_ref[plane_of.index(plane)], plane_rows)
                term = lax.dot_general(
                    rows[g][here, (plane - first) * plane_rows : (plane + 1 - first) * plane_rows],
                    vector_ref[own_vectors + i, :, pl.ds(start, plane_rows)],
                    (((1,), (1,)), ((), ())),
                    preferred_element_type=jnp.float32,
                )
                vector = term if vector is None else vector + term
            for part in range(2):
                at = slice(part * columns, (part + 1) * columns)
                value = values[part][here]
                if base is not None:
                    value += totals[g][here, at].astype(jnp.float32)
                if ranked and own_vectors is None:
                    value += sigma_perturb * proj_ref[there, part : part + 1] * col_ref[part, member : member + 1, :]
                if vector is not None:
                    value += sigma_perturb * vector[:, part : part + 1] * vector_col_ref[part, own_vectors + i]
                if not read_out:
                    totals[g][here, at] = value.astype(jnp.bfloat16)
                found.append(value)
            if read_out:
                gate, up = found
                hidden = (0.5 * gate * (1.0 + jnp.tanh(0.5 * gate)) * up).astype(jnp.bfloat16)
                terms = hidden.astype(jnp.float32) * head
                out_ref[member] = jnp.sum(terms.reshape(seq // 8, 8, columns), axis=0)
        if not read_out:
            target = out_ref.at[pl.ds(done_rows, count)]
            out_copies.append(pltpu.make_async_copy(totals[g], target, total_sems.at[g]))
            out_copies[-1].start()
        done_rows += count
    for copy in out_copies:
        copy.wait()


def product(groups, seq, chunks, ranks=(), vectors=(), read_out=()):
    columns = chunks[0][3].shape[2]
    arrays, base_arrays, plan = [], [], []

    def number(array, known):
        for i, other in enumerate(known):
            if other is array:
                return i
        known.append(array)
        return len(known) - 1

    for segments, first, base, own_vectors in groups:
        placed = [(number(a, arrays), row, rows) for a, row, rows in segments]
        plan.append((placed, first, base and (number(base[0], base_arrays), base[1]), own_vectors))
    sizes = [sum(rows for _, _, rows in segments) for segments, _, _, _ in groups]
    total = sum(sizes)
    keys = list(dict.fromkeys(key for key, _, _, _ in chunks))
    plane_of = [keys.index(key) for key, _, _, _ in chunks]
    plane_rows = sum(chunk.shape[1] for key, _, _, chunk in chunks if key == keys[0])
    counts = [len(arrays), len(chunks), len(base_arrays)]
    buffers = [pltpu.VMEM((2, len(keys) * plane_rows, columns), jnp.bfloat16)]
    for (_, first, base, _), size in zip(groups, sizes):
        buffers.append(pltpu.VMEM((size, (len(keys) - first) * plane_rows), jnp.bfloat16))
        if base is not None or not read_out:
            buffers.append(pltpu.VMEM((size, 2 * columns), jnp.bfloat16))
    given = [*arrays, *[chunk for _, _, _, chunk in chunks], *base_arrays]
    given = [pltpu.with_memory_space_constraint(a, pltpu.HBM) for a in given]
    extra = [*ranks, *vectors, *read_out]
    held = sum(2 * math.prod(b.shape) for b in buffers) + 4 * total * columns
    held += sum(4 * 128 * a.size // min(128, a.shape[-1]) for a in extra)
    vmem = pl.BlockSpec(memory_space=pltpu.VMEM)
    outside = pl.BlockSpec(memory_space=pl.ANY)
    shape = pltpu.HBM((total, 2 * columns), jnp.bfloat16)
    if read_out:
        shape = jax.ShapeDtypeStruct((total // seq, 8, columns), jnp.float32)
    parts = max(len(segments) for segments, _, _, _ in groups)
    return pl.pallas_call(
        lambda *refs: product_kernel(plan, counts, plane_of, seq, bool(ranks), bool(vectors), bool(read_out), *refs),
        out_shape=shape,
        in_specs=[pl.BlockSpec(memory_space=pltpu.SMEM)] + [outside] * len(given) + [vmem] * len(extra),
        out_specs=vmem if read_out else outside,
        scratch_shapes=[
            *buffers,
            pltpu.SemaphoreType.DMA((len(groups), parts, len(keys))),
            pltpu.SemaphoreType.DMA((len(chunks),)),
            pltpu.SemaphoreType.DMA((len(groups),)),
        ],
        compiler_params=pltpu.CompilerParams(vmem_limit_bytes=held + SPARE_BYTES),
        cost_estimate=pl.CostEstimate(flops=1, bytes_accessed=1, transcendentals=0),
    )(jnp.stack([c[1] for c in chunks] + [c[2] for c in chunks]), *given, *extra)


def tree_sum(terms):
    while len(terms) > 1:
        half = len(terms) // 2
        terms = [terms[i] + terms[i + half] for i in range(half)]
    return terms[0]


def spread_plan(planes, prompts, gate_weight, up_weight, reward_head, member_seeds, counters, member_ranks):
    members_here, seq, width = prompts.shape
    own_rows, own_cols = gate_weight.shape
    n_mp = members_here
    pop_index = lax.axis_index("pop")
    mp_index = lax.axis_index("mp")
    z, core = pop_index // CORES, pop_index % CORES
    block = own_cols // planes

    def pairs(move, keep=lambda z: True):
        out = []
        for a in range(planes):
            for c in range(CORES):
                for m in range(n_mp):
                    target = move(a, c, m)
                    if keep(a) and 0 <= target[0] < planes:
                        source = (a * CORES + c) * n_mp + m
                        out.append((source, (target[0] * CORES + target[1]) * n_mp + target[2]))
        return out

    def send(value, move, keep=lambda z: True):
        return lax.ppermute(value, AXES, pairs(move, keep))

    def swap_core(value):
        return send(value, lambda a, c, m: (a, 1 - c, m))

    def swap_in_plane(value, bit):
        return send(value, lambda a, c, m: (a, c, m ^ bit))

    def turn(value, s):
        return send(value, lambda a, c, m: ((a + s) % planes, c, m))

    def tie(*values):
        return lax.optimization_barrier(values)

    def up(value, s):
        return send(value, lambda a, c, m: (a + 1, c, m), lambda a: a >= s - 1)

    def down(value, s):
        return send(value, lambda a, c, m: (a - 1, c, m), lambda a: a <= planes - s)

    arrivals = []
    for a in range(planes):
        order = []
        for s in range(1, planes):
            if a - s >= 0:
                order.append((0, s, a - s))
            if a + s < planes:
                order.append((1, s, a + s))
        arrivals.append(order)

    def by_plane(numbers):
        value = jnp.int32(numbers[0])
        for a in range(1, planes):
            value = jnp.where(z == a, numbers[a], value)
        return value

    def round_block(r):
        picks = {}
        for a in range(planes):
            picks.setdefault(arrivals[a][r - 1][:2], []).append(a)
        chosen = None
        for (way, s), where in picks.items():
            here = z == where[0]
            for a in where[1:]:
                here = here | (z == a)
            value = hops[way][s]
            chosen = value if chosen is None else jnp.where(here, value, chosen)
        return chosen

    def piece(weights, s, first, count):
        corner = (first, (z + s) % planes * block)
        return jnp.stack([lax.dynamic_slice(w, corner, (count, block)) for w in weights])

    small = jnp.stack([member_seeds, counters, member_ranks])
    own_member = lax.dynamic_index_in_dim(prompts, mp_index, 0, keepdims=False)
    hops = [[own_member, up(own_member, 1)], [own_member, down(own_member, 1)]]
    small_here = jnp.stack([small] + [turn(small, s) for s in range(1, planes)])
    small_other = swap_core(small_here)
    every = jnp.concatenate([small_here, small_other]).transpose(1, 0, 2).reshape(3, -1)
    head = lax.dynamic_slice_in_dim(reward_head, z * block, block).reshape(1, block)
    my_columns = mp_index * own_cols + z * block + jnp.arange(block, dtype=jnp.int32)
    positions = jnp.arange(width, dtype=jnp.int32)
    lanes = jnp.arange(members_here, dtype=jnp.int32)

    rel = mp_index ^ lanes
    rel_hot = (rel[:, None] == lanes[None, :]).astype(jnp.int32)
    flat = prompts.reshape(members_here * seq, width)
    members = [[(flat, i * seq, seq)] for i in range(members_here)]
    group_ids = [pop_index * members_here + lanes]
    picked = [(member_seeds, counters)]
    for r in range(1, planes):
        source = by_plane([arrivals[a][r - 1][2] for a in range(planes)])
        back = (z - source) % planes
        chosen = jnp.int32(0)
        for s in range(1, planes):
            chosen = jnp.where(back == s, small_here[s], chosen)
        chosen = jnp.sum(rel_hot[None] * chosen[:, None, :], axis=2)
        picked.append((chosen[0], chosen[1]))
        group_ids.append((source * CORES + core) * members_here + rel)

    def new_vectors(r):
        seeds, counts = picked[r]
        return jnp.stack(
            [factor_rows(seeds, counts + 1, slot, positions).astype(jnp.bfloat16) for slot in (0, 2)],
            axis=1,
        )

    def projected(r, vectors, some):
        found = []
        for i in some:
            parts = [
                lax.dot_general(
                    array[first : first + rows],
                    vectors[i],
                    (((1,), (1,)), ((), ())),
                    preferred_element_type=jnp.float32,
                )
                for array, first, rows in members[r * members_here + i]
            ]
            found.append(parts[0] if len(parts) == 1 else jnp.concatenate(parts))
        return found

    cols = [
        jnp.stack([factor_rows(seeds, counts + 1, slot + 1, my_columns) for slot in (0, 2)])
        for seeds, counts in picked
    ]
    cols = jnp.concatenate(cols, axis=1)
    vectors = [new_vectors(r) for r in range(planes)]
    late_vectors = jnp.concatenate([vectors[planes - 2][members_here - 1 :], vectors[planes - 1]])
    late_vectors = jnp.pad(late_vectors, ((0, 0), (0, 14), (0, 0)))
    late = (late_vectors, cols[:, (planes - 1) * members_here - 1 :, None])
    projs = projected(0, vectors[0], range(members_here))

    column_ids = mp_index * own_cols + jnp.arange(own_cols, dtype=jnp.int32)
    weights = fresh_weights(
        gate_weight, up_weight, every[0], every[1], every[2], pop_index * own_rows, column_ids
    )
    new_gate, new_up = weights
    far_first = sorted(range(1, planes), key=lambda s: (-min(s, planes - s), s))
    half_rows = own_rows // 2
    queue = [(s, 0, own_rows) for s in far_first[:-1]]
    queue += [(far_first[-1], first, half_rows) for first in (0, half_rows)]
    leave = {planes - 2: queue[:1], planes - 1: queue[1:-1], planes: queue[-1:]}
    outgoing = {key: piece(weights, *key) for key in queue}
    landed = {(0, 0, own_rows): piece(weights, 0, 0, own_rows)}
    chunks = []

    def add_chunks(key):
        s, first, _ = key
        start = (z - s) % planes * CORES * own_rows
        return [
            (s, start, core * own_rows + first, landed[key]),
            (s, start, (1 - core) * own_rows + first, swap_core(landed[key])),
        ]

    half = seq // 2
    fresh = [(0, 0, own_rows)]
    base, early, early_planes = None, 0, 0

    def on(some, first, base=None, vectors=None):
        groups = []
        for i in range(0, len(some), members_here):
            segments = []
            for segment in [s for m in some[i : i + members_here] for s in m]:
                array, row, rows = segments[-1] if segments else (None, 0, 0)
                if array is segment[0] and row + rows == segment[1]:
                    segments[-1] = (array, row, rows + segment[2])
                else:
                    segments.append(segment)
            groups.append((segments, first, None if base is None else (base, i * seq), vectors if vectors is None else vectors + i))
        return groups

    next_here = round_block(1)
    to_x, to_y, hops[0][1], hops[1][1] = tie(next_here, next_here, hops[0][1], hops[1][1])
    next_here = to_x
    for phase in range(1, planes + 1):
        if phase < planes - 1:
            hops[0].append(up(hops[0][phase], phase + 1))
            hops[1].append(down(hops[1][phase], phase + 1))
        if phase < planes:
            here = next_here
        new_x = swap_in_plane(to_x, 1)
        new_y = swap_in_plane(to_y, 2)
        for key in leave.get(phase, ()):
            landed[key] = turn(outgoing[key], key[0])
        new_chunks = [c for key in fresh for c in add_chunks(key)]
        fresh = leave.get(phase, ())
        known = chunks + new_chunks
        if phase == planes - 1:
            early, early_planes = len(members), len(set(c[0] for c in known))
            ranks = (jnp.concatenate(projs), cols[:, :early])
            base = product(on(members, 0), seq, known, ranks)
        elif phase == planes:
            landed_first = [c for c in chunks + new_chunks if c[0] != far_first[-1]]
            groups = on(members[:early], early_planes, base) + on(members[early:], 0, None, 0)
            base = product(groups, seq, landed_first, (), late)
        def next_sends():
            to_x, to_y, here = [new_y[:half]], [new_x[half:seq]], None
            if phase + 1 < planes:
                here = round_block(phase + 1)
                to_x, to_y = [here, *to_x], [here, *to_y]
            return jnp.concatenate(to_x), jnp.concatenate(to_y), here

        ahead = ()
        if phase in leave and phase < planes:
            hops, new_x, new_y = tie(hops, new_x, new_y)
            ahead = next_sends()
        held = [chunk for _, _, _, chunk in new_chunks]
        parts = (hops, new_x, new_y, ahead, landed, held, outgoing, base, cols, late, projs, head)
        hops, new_x, new_y, ahead, landed, held, outgoing, base, cols, late, projs, head = tie(*parts)
        if phase < planes:
            to_x, to_y, next_here = ahead or next_sends()
        chunks += [(*c[:3], chunk) for c, chunk in zip(new_chunks, held)]
        if phase > 1:
            first = seq if phase < planes else 0
            members.append([(new_x, first, half), (new_y, first, half)])
        if 1 < phase < planes - 1:
            projs += projected(phase - 1, vectors[phase - 1], [members_here - 1])
        if phase < planes:
            members += [[(here, 0, seq)], [(new_x, 0, seq)], [(new_y, 0, seq)]]
        if phase < planes - 1:
            projs += projected(phase, vectors[phase], range(members_here - 1))

    last = [c for key in fresh for c in add_chunks(key)]
    plan = on(members[:early], planes - 1, base)
    plan += [
        (segments, first, (base, early * seq + row), here)
        for segments, first, (_, row), here in on(members[early:-1], planes - 1, base, 0)
    ]
    plan += on(members[-1:], 0, None, len(members) - 1 - early)
    sums = product(plan, seq, chunks + last, (), late, (head,))
    sums = sums.reshape(len(members), -1).sum(axis=1)

    ids = jnp.concatenate(group_ids)
    total = planes * CORES * members_here
    rewards = jnp.sum(
        jnp.where(ids[:, None] == jnp.arange(total, dtype=jnp.int32)[None, :], sums[:, None], 0.0),
        axis=0,
    ).reshape(1, total)
    rewards = (rewards + swap_in_plane(rewards, 1)) + (
        swap_in_plane(rewards, 2) + swap_in_plane(rewards, 3)
    )
    rewards = tree_sum([rewards] + [turn(rewards, s) for s in range(1, planes)])
    rewards = (rewards + swap_core(rewards)).reshape(total) / seq
    own = lax.dynamic_slice_in_dim(normalized(rewards), pop_index * members_here, members_here)
    return new_gate, new_up, own


def solution(mesh):
    n_pop, n_mp = mesh.shape["pop"], mesh.shape["mp"]
    planes = n_pop // CORES

    def shards(prompts, gate_weight, *rest):
        members_here, seq, width = prompts.shape
        own_cols = gate_weight.shape[1]
        gathered = 2 * width * own_cols + members_here * seq * width
        spread = 2 * width * own_cols // planes + planes * members_here * seq * width
        square = n_mp == 4 and members_here == n_mp and planes & (planes - 1) == 0
        if square and own_cols % (128 * planes) == 0 and spread < gathered:
            return spread_plan(planes, prompts, gate_weight, *rest)
        return gathered_plan(prompts, gate_weight, *rest)

    in_specs = (
        P("pop", None, None),
        P("pop", "mp"),
        P("pop", "mp"),
        P("mp"),
        P("pop"),
        P("pop"),
        P("pop"),
    )
    out_specs = (P("pop", "mp"), P("pop", "mp"), P("pop"))
    return jax.shard_map(shards, mesh=mesh, in_specs=in_specs, out_specs=out_specs, check_vma=False)
```

```python
import math

import jax
import jax.numpy as jnp
from jax import lax
from jax.experimental import pallas as pl
from jax.experimental.pallas import tpu as pltpu
from jax.sharding import PartitionSpec as P

sigma_perturb = 0.004
learn_rate = 0.0016
AXES = ("pop", "mp")
CORES = 2
FIRST_STAGES, NEXT_STAGES = 2, 1
SPARE_BYTES = 4 * 1024 * 1024


def shift_down(number, amount):
    return lax.shift_right_logical(number, jnp.full_like(number, amount))


def mix_bits(number):
    number = number ^ shift_down(number, 16)
    number = number * 2146121005
    number = number ^ shift_down(number, 15)
    number = number * -2073254261
    return number ^ shift_down(number, 16)


def factor_rows(seed_list, counter_list, slot, positions):
    anchor = mix_bits(
        seed_list * 1103515245 + mix_bits(counter_list * 668265263 + slot * 374761393)
    )
    hashed = mix_bits(anchor[:, None] + positions[None, :] * -1640531535)
    uniform_part = shift_down(hashed, 8).astype(jnp.float32) * (1.0 / 16777216.0)
    return (2.0 * uniform_part - 1.0 + 1.0 / 16777216.0) * 1.7320508075688772


def fresh_weights(gate_weight, up_weight, seeds, counters, ranks, row_start, column_ids):
    members_all = seeds.shape[0]
    fitness = (ranks.astype(jnp.float32) + 0.5) / members_all - 0.5
    scaling = learn_rate / (members_all * sigma_perturb)
    row_ids = row_start + jnp.arange(gate_weight.shape[0], dtype=jnp.int32)

    def fresh(weight, slot):
        right = factor_rows(seeds, counters, slot + 1, column_ids).astype(jnp.bfloat16)
        left = (factor_rows(seeds, counters, slot, row_ids) * fitness[:, None]).astype(jnp.bfloat16)
        update = scaling * jnp.dot(left.T, right, preferred_element_type=jnp.float32)
        return (weight.astype(jnp.float32) + update).astype(jnp.bfloat16)

    return fresh(gate_weight, 0), fresh(up_weight, 2)


def normalized(rewards):
    reward_mean = jnp.mean(rewards)
    reward_var = jnp.mean((rewards - reward_mean) ** 2)
    return (rewards - reward_mean) / jnp.sqrt(reward_var + 1e-05)


def gathered_plan(
    prompts, gate_weight, up_weight, reward_head, member_seeds, counters, member_ranks
):
    members_here, seq_len, width = prompts.shape
    own_rows, own_cols = gate_weight.shape
    pop_index = lax.axis_index("pop")
    column_ids = lax.axis_index("mp") * own_cols + jnp.arange(own_cols, dtype=jnp.int32)
    small = lax.all_gather(
        jnp.stack([member_seeds, counters, member_ranks]), "pop", axis=1, tiled=True
    )
    new_gate, new_up = fresh_weights(
        gate_weight, up_weight, small[0], small[1], small[2], pop_index * own_rows, column_ids
    )
    flat_rows = prompts.reshape(members_here * seq_len, width)
    later = counters + 1
    positions = jnp.arange(width, dtype=jnp.int32)

    def projected(weight, slot):
        base = jnp.dot(
            flat_rows,
            lax.all_gather(weight, "pop", axis=0, tiled=True),
            preferred_element_type=jnp.float32,
        ).reshape(members_here, seq_len, own_cols)
        vector = factor_rows(member_seeds, later, slot, positions).astype(jnp.bfloat16)
        column = factor_rows(member_seeds, later, slot + 1, column_ids)
        proj = jnp.einsum("mld,md->ml", prompts, vector, preferred_element_type=jnp.float32)
        return base + sigma_perturb * proj[:, :, None] * column[:, None, :]

    hidden = (jax.nn.silu(projected(new_gate, 0)) * projected(new_up, 2)).astype(jnp.bfloat16)
    partial = jnp.einsum("mlf,f->m", hidden, reward_head, preferred_element_type=jnp.float32)
    rewards = lax.all_gather(lax.psum(partial, "mp"), "pop", axis=0, tiled=True) / seq_len
    own = lax.dynamic_slice_in_dim(normalized(rewards), pop_index * members_here, members_here)
    return new_gate, new_up, own


def product_kernel(plan, counts, plane_of, seq, ranked, vectored, read_out, starts_ref, *refs):
    refs = list(refs)
    x_refs, w_refs, base_refs = [[refs.pop(0) for _ in range(count)] for count in counts]
    if ranked:
        proj_ref, col_ref = refs.pop(0), refs.pop(0)
    if vectored:
        vector_ref, vector_col_ref = refs.pop(0), refs.pop(0)
    if read_out:
        head_ref = refs.pop(0)
        head = head_ref[...].astype(jnp.float32)
    out_ref, weights = refs.pop(0), refs.pop(0)
    rows, totals = [], []
    for _, _, base, _ in plan:
        rows.append(refs.pop(0))
        totals.append(refs.pop(0) if base is not None or not read_out else None)
    row_sems, weight_sems, total_sems = refs
    columns = weights.shape[2]
    n_planes = 1 + plane_of[-1]
    plane_rows = weights.shape[1] // n_planes
    weight_copies = []
    for k, w_ref in enumerate(w_refs):
        depth = w_ref.shape[1]
        at = plane_of[k] * plane_rows + pl.multiple_of(starts_ref[len(w_refs) + k], depth)
        weight_copies.append(pltpu.make_async_copy(w_ref, weights.at[:, pl.ds(at, depth)], weight_sems.at[k]))
    group_copies = []
    for g, (segments, first, base, _) in enumerate(plan):
        copies = []
        row = 0
        for i, (x, start_row, count) in enumerate(segments):
            for plane in range(first, n_planes):
                start = pl.multiple_of(starts_ref[plane_of.index(plane)], plane_rows)
                copies.append(
                    pltpu.make_async_copy(
                        x_refs[x].at[pl.ds(start_row, count), pl.ds(start, plane_rows)],
                        rows[g].at[pl.ds(row, count), pl.ds((plane - first) * plane_rows, plane_rows)],
                        row_sems.at[g, i, plane],
                    )
                )
            row += count
        if base is not None:
            source = base_refs[base[0]].at[pl.ds(base[1], row)]
            copies.append(pltpu.make_async_copy(source, totals[g], total_sems.at[g]))
        group_copies.append(copies)
    taken, stages = set(), []
    for g, (_, first, _, _) in enumerate(plan):
        fresh = [k for k in range(len(w_refs)) if plane_of[k] >= first and k not in taken]
        taken.update(fresh)
        stages.append([weight_copies[k] for k in fresh] + group_copies[g])
    queue = list(stages)

    def start_stages(count):
        for copy in [c for stage in queue[:count] for c in stage]:
            copy.start()
        del queue[:count]

    start_stages(FIRST_STAGES)
    done_rows, out_copies = 0, []
    for g, (_, first, base, own_vectors) in enumerate(plan):
        for copy in stages[g]:
            copy.wait()
        start_stages(NEXT_STAGES)
        count = rows[g].shape[0]
        values = [
            jnp.dot(rows[g][...], weights[part, first * plane_rows :], preferred_element_type=jnp.float32)
            for part in range(2)
        ]
        for i in range(count // seq):
            here = slice(i * seq, (i + 1) * seq)
            there = slice(done_rows + i * seq, done_rows + (i + 1) * seq)
            member = done_rows // seq + i
            found = []
            vector = None
            for plane in range(first, n_planes if own_vectors is not None else first):
                start = pl.multiple_of(starts_ref[plane_of.index(plane)], plane_rows)
                term = lax.dot_general(
                    rows[g][here, (plane - first) * plane_rows : (plane + 1 - first) * plane_rows],
                    vector_ref[own_vectors + i, :, pl.ds(start, plane_rows)],
                    (((1,), (1,)), ((), ())),
                    preferred_element_type=jnp.float32,
                )
                vector = term if vector is None else vector + term
            for part in range(2):
                at = slice(part * columns, (part + 1) * columns)
                value = values[part][here]
                if base is not None:
                    value += totals[g][here, at].astype(jnp.float32)
                if ranked and own_vectors is None:
                    value += sigma_perturb * proj_ref[there, part : part + 1] * col_ref[part, member : member + 1, :]
                if vector is not None:
                    value += sigma_perturb * vector[:, part : part + 1] * vector_col_ref[part, own_vectors + i]
                if not read_out:
                    totals[g][here, at] = value.astype(jnp.bfloat16)
                found.append(value)
            if read_out:
                gate, up = found
                half = 0.5 * gate
                hidden = (half + half * jnp.tanh(half)) * up
                out_ref[member] = jnp.sum(hidden.reshape(seq // 8, 8, columns), axis=0) * head
        if not read_out:
            target = out_ref.at[pl.ds(done_rows, count)]
            out_copies.append(pltpu.make_async_copy(totals[g], target, total_sems.at[g]))
            out_copies[-1].start()
        done_rows += count
    for copy in out_copies:
        copy.wait()


def product(groups, seq, chunks, ranks=(), vectors=(), read_out=()):
    columns = chunks[0][3].shape[2]
    arrays, base_arrays, plan = [], [], []

    def number(array, known):
        for i, other in enumerate(known):
            if other is array:
                return i
        known.append(array)
        return len(known) - 1

    for segments, first, base, own_vectors in groups:
        placed = [(number(a, arrays), row, rows) for a, row, rows in segments]
        plan.append((placed, first, base and (number(base[0], base_arrays), base[1]), own_vectors))
    sizes = [sum(rows for _, _, rows in segments) for segments, _, _, _ in groups]
    total = sum(sizes)
    keys = list(dict.fromkeys(key for key, _, _, _ in chunks))
    plane_of = [keys.index(key) for key, _, _, _ in chunks]
    plane_rows = sum(chunk.shape[1] for key, _, _, chunk in chunks if key == keys[0])
    counts = [len(arrays), len(chunks), len(base_arrays)]
    buffers = [pltpu.VMEM((2, len(keys) * plane_rows, columns), jnp.bfloat16)]
    for (_, first, base, _), size in zip(groups, sizes):
        buffers.append(pltpu.VMEM((size, (len(keys) - first) * plane_rows), jnp.bfloat16))
        if base is not None or not read_out:
            buffers.append(pltpu.VMEM((size, 2 * columns), jnp.bfloat16))
    far = [pltpu.with_memory_space_constraint(a, pltpu.HBM) for a in [*arrays, *base_arrays]]
    near = [chunk for _, _, _, chunk in chunks]
    near[::2] = [pltpu.with_memory_space_constraint(a, pltpu.HBM) for a in near[::2]]
    given = [*far[: len(arrays)], *near, *far[len(arrays) :]]
    extra = [*ranks, *vectors, *read_out]
    held = sum(2 * math.prod(b.shape) for b in buffers) + 4 * total * columns
    held += sum(4 * 128 * a.size // min(128, a.shape[-1]) for a in extra)
    vmem = pl.BlockSpec(memory_space=pltpu.VMEM)
    outside = pl.BlockSpec(memory_space=pl.ANY)
    shape = pltpu.HBM((total, 2 * columns), jnp.bfloat16)
    if read_out:
        shape = jax.ShapeDtypeStruct((total // seq, 8, columns), jnp.float32)
    parts = max(len(segments) for segments, _, _, _ in groups)
    return pl.pallas_call(
        lambda *refs: product_kernel(plan, counts, plane_of, seq, bool(ranks), bool(vectors), bool(read_out), *refs),
        out_shape=shape,
        in_specs=[pl.BlockSpec(memory_space=pltpu.SMEM)] + [outside] * len(given) + [vmem] * len(extra),
        out_specs=vmem if read_out else outside,
        scratch_shapes=[
            *buffers,
            pltpu.SemaphoreType.DMA((len(groups), parts, len(keys))),
            pltpu.SemaphoreType.DMA((len(chunks),)),
            pltpu.SemaphoreType.DMA((len(groups),)),
        ],
        compiler_params=pltpu.CompilerParams(vmem_limit_bytes=held + SPARE_BYTES),
        cost_estimate=pl.CostEstimate(flops=1, bytes_accessed=1, transcendentals=0),
    )(jnp.stack([c[1] for c in chunks] + [c[2] for c in chunks]), *given, *extra)


def tree_sum(terms):
    while len(terms) > 1:
        half = len(terms) // 2
        terms = [terms[i] + terms[i + half] for i in range(half)]
    return terms[0]


def own_scores(first, second, start, count, seq):
    def kernel(start_ref, first_ref, second_ref, out_ref):
        rewards = (first_ref[...] + second_ref[...]) / seq
        total = rewards.shape[1]
        mean = jnp.sum(rewards, axis=1, keepdims=True) / total
        spread = jnp.sum((rewards - mean) ** 2, axis=1, keepdims=True) / total
        scores = (rewards - mean) / jnp.sqrt(spread + 1e-05)
        places = lax.broadcasted_iota(jnp.int32, (count, total), 1)
        wanted = start_ref[0] + lax.broadcasted_iota(jnp.int32, (count, total), 0)
        column = jnp.sum(jnp.where(places == wanted, scores, 0.0), axis=1, keepdims=True)
        row, lane = [lax.broadcasted_iota(jnp.int32, (count, count), axis) for axis in range(2)]
        out_ref[...] = jnp.sum(jnp.where(row == lane, column, 0.0), axis=0, keepdims=True)

    vmem = pl.BlockSpec(memory_space=pltpu.VMEM)
    return pl.pallas_call(
        kernel,
        out_shape=jax.ShapeDtypeStruct((1, count), jnp.float32),
        in_specs=[pl.BlockSpec(memory_space=pltpu.SMEM), vmem, vmem],
        out_specs=vmem,
    )(start.reshape(1), *[pltpu.with_memory_space_constraint(a, pltpu.VMEM) for a in (first, second)]).reshape(count)


def spread_plan(planes, prompts, gate_weight, up_weight, reward_head, member_seeds, counters, member_ranks):
    members_here, seq, width = prompts.shape
    own_rows, own_cols = gate_weight.shape
    n_mp = members_here
    pop_index = lax.axis_index("pop")
    mp_index = lax.axis_index("mp")
    z, core = pop_index // CORES, pop_index % CORES
    block = own_cols // planes

    def pairs(move, keep=lambda z: True):
        out = []
        for a in range(planes):
            for c in range(CORES):
                for m in range(n_mp):
                    target = move(a, c, m)
                    if keep(a) and 0 <= target[0] < planes:
                        source = (a * CORES + c) * n_mp + m
                        out.append((source, (target[0] * CORES + target[1]) * n_mp + target[2]))
        return out

    def send(value, move, keep=lambda z: True):
        return lax.ppermute(value, AXES, pairs(move, keep))

    def swap_core(value):
        return send(value, lambda a, c, m: (a, 1 - c, m))

    def swap_in_plane(value, bit):
        return send(value, lambda a, c, m: (a, c, m ^ bit))

    def turn(value, s):
        return send(value, lambda a, c, m: ((a + s) % planes, c, m))

    def tie(*values):
        return lax.optimization_barrier(values)

    def up(value, s):
        return send(value, lambda a, c, m: (a + 1, c, m), lambda a: a >= s - 1)

    def down(value, s):
        return send(value, lambda a, c, m: (a - 1, c, m), lambda a: a <= planes - s)

    arrivals = []
    for a in range(planes):
        order = []
        for s in range(1, planes):
            if a - s >= 0:
                order.append((0, s, a - s))
            if a + s < planes:
                order.append((1, s, a + s))
        arrivals.append(order)

    def by_plane(numbers):
        value = jnp.int32(numbers[0])
        for a in range(1, planes):
            value = jnp.where(z == a, numbers[a], value)
        return value

    def round_block(r):
        picks = {}
        for a in range(planes):
            picks.setdefault(arrivals[a][r - 1][:2], []).append(a)
        chosen = None
        for (way, s), where in picks.items():
            here = z == where[0]
            for a in where[1:]:
                here = here | (z == a)
            value = hops[way][s]
            chosen = value if chosen is None else jnp.where(here, value, chosen)
        return chosen

    def piece(weights, s, first, count):
        corner = (first, (z + s) % planes * block)
        return jnp.stack([lax.dynamic_slice(w, corner, (count, block)) for w in weights])

    small = jnp.stack([member_seeds, counters, member_ranks])
    own_member = lax.dynamic_index_in_dim(prompts, mp_index, 0, keepdims=False)
    own_member, small = tie(own_member, small)
    hops = [[own_member, up(own_member, 1)], [own_member, down(own_member, 1)]]
    small_here = jnp.stack([small] + [turn(small, s) for s in range(1, planes)])
    small_other = swap_core(small_here)
    every = jnp.concatenate([small_here, small_other]).transpose(1, 0, 2).reshape(3, -1)
    head = lax.dynamic_slice_in_dim(reward_head, z * block, block).reshape(1, block)
    my_columns = mp_index * own_cols + z * block + jnp.arange(block, dtype=jnp.int32)
    positions = jnp.arange(width, dtype=jnp.int32)
    lanes = jnp.arange(members_here, dtype=jnp.int32)

    rel = mp_index ^ lanes
    rel_hot = (rel[:, None] == lanes[None, :]).astype(jnp.int32)
    flat = prompts.reshape(members_here * seq, width)
    members = [[(flat, i * seq, seq)] for i in range(members_here)]
    group_ids = [pop_index * members_here + lanes]
    picked = [(member_seeds, counters)]
    for r in range(1, planes):
        source = by_plane([arrivals[a][r - 1][2] for a in range(planes)])
        back = (z - source) % planes
        chosen = jnp.int32(0)
        for s in range(1, planes):
            chosen = jnp.where(back == s, small_here[s], chosen)
        chosen = jnp.sum(rel_hot[None] * chosen[:, None, :], axis=2)
        picked.append((chosen[0], chosen[1]))
        group_ids.append((source * CORES + core) * members_here + rel)

    def new_vectors(r):
        seeds, counts = picked[r]
        return jnp.stack(
            [factor_rows(seeds, counts + 1, slot, positions).astype(jnp.bfloat16) for slot in (0, 2)],
            axis=1,
        )

    def on_vector(rows, vector):
        return lax.dot_general(
            rows, vector, (((1,), (1,)), ((), ())), preferred_element_type=jnp.float32
        )

    def projected(r, vectors, some):
        found = []
        for i in some:
            parts = [
                on_vector(array[first : first + rows], vectors[i])
                for array, first, rows in members[r * members_here + i]
            ]
            found.append(parts[0] if len(parts) == 1 else jnp.concatenate(parts))
        return found

    cols = [
        jnp.stack([factor_rows(seeds, counts + 1, slot + 1, my_columns) for slot in (0, 2)])
        for seeds, counts in picked
    ]
    cols = jnp.concatenate(cols, axis=1)
    vectors = [new_vectors(r) for r in range(planes)]
    late_vectors = jnp.concatenate([vectors[planes - 2][members_here - 1 :], vectors[planes - 1]])
    late_vectors = jnp.pad(late_vectors, ((0, 0), (0, 14), (0, 0)))
    late = (late_vectors, cols[:, (planes - 1) * members_here - 1 :, None])
    projs = projected(0, vectors[0], range(members_here))

    column_ids = mp_index * own_cols + jnp.arange(own_cols, dtype=jnp.int32)
    weights = fresh_weights(
        gate_weight, up_weight, every[0], every[1], every[2], pop_index * own_rows, column_ids
    )
    new_gate, new_up = weights
    far_first = sorted(range(1, planes), key=lambda s: (-min(s, planes - s), s))
    half_rows = own_rows // 2
    queue = [(s, 0, own_rows) for s in far_first[:-1]]
    queue += [(far_first[-1], first, half_rows) for first in (0, half_rows)]
    leave = {planes - 2: queue[:1], planes - 1: queue[1:-1], planes: queue[-1:]}
    outgoing = {key: piece(weights, *key) for key in queue}
    landed = {(0, 0, own_rows): piece(weights, 0, 0, own_rows)}
    chunks = []

    def add_chunks(key):
        s, first, _ = key
        start = (z - s) % planes * CORES * own_rows
        return [
            (s, start, core * own_rows + first, landed[key]),
            (s, start, (1 - core) * own_rows + first, swap_core(landed[key])),
        ]

    half = seq // 2
    fresh = [(0, 0, own_rows)]
    base, early, early_planes, waiting = None, 0, 0, 0

    def on(some, first, base=None, vectors=None):
        groups = []
        for i in range(0, len(some), members_here):
            segments = []
            for segment in [s for m in some[i : i + members_here] for s in m]:
                array, row, rows = segments[-1] if segments else (None, 0, 0)
                if array is segment[0] and row + rows == segment[1]:
                    segments[-1] = (array, row, rows + segment[2])
                else:
                    segments.append(segment)
            groups.append((segments, first, None if base is None else (base, i * seq), vectors if vectors is None else vectors + i))
        return groups

    hops[0][1], hops[1][1] = tie(hops[0][1], hops[1][1])
    to_x = to_y = next_here = round_block(1)
    for phase in range(1, planes + 1):
        if phase < planes - 1:
            hops[0].append(up(hops[0][phase], phase + 1))
            hops[1].append(down(hops[1][phase], phase + 1))
        if phase < planes:
            here = next_here
        new_x = swap_in_plane(to_x, 1)
        new_y = swap_in_plane(to_y, 2)
        for key in leave.get(phase, ()):
            landed[key] = turn(outgoing[key], key[0])
        new_chunks = [c for key in fresh for c in add_chunks(key)]
        fresh = leave.get(phase, ())
        known = chunks + new_chunks
        if phase == planes - 1:
            early, early_planes = len(members), len(set(c[0] for c in known))
            ranks = (jnp.concatenate(projs), cols[:, :early])
            base = product(on(members, 0), seq, known, ranks)
        elif phase == planes:
            landed_first = [c for c in chunks + new_chunks if c[0] != far_first[-1]]
            groups = on(members[:early], early_planes, base) + on(members[early:], 0, None, 0)
            base = product(groups, seq, landed_first, (), late)
        def next_sends():
            to_x, to_y, here = [new_y[:half]], [new_x[half:seq]], None
            if phase + 1 < planes:
                here = round_block(phase + 1)
                to_x, to_y = [here, *to_x], [here, *to_y]
            return jnp.concatenate(to_x), jnp.concatenate(to_y), here

        ahead = ()
        if phase in leave and phase < planes:
            held = [members[waiting * members_here + i][0][0] for i in range(members_here - 1) if waiting]
            hops, new_x, new_y, held = tie(hops, new_x, new_y, held)
            ahead = next_sends()
            projs += [on_vector(array, vectors[waiting][i]) for i, array in enumerate(held)]
            waiting = 0
        held = [chunk for _, _, _, chunk in new_chunks]
        parts = (hops, new_x, new_y, ahead, landed, held, outgoing, base, cols, late, projs, head)
        hops, new_x, new_y, ahead, landed, held, outgoing, base, cols, late, projs, head = tie(*parts)
        if phase < planes:
            to_x, to_y, next_here = ahead or next_sends()
        chunks += [(*c[:3], chunk) for c, chunk in zip(new_chunks, held)]
        if phase > 1:
            first = seq if phase < planes else 0
            members.append([(new_x, first, half), (new_y, first, half)])
        if 1 < phase < planes - 1:
            projs += projected(phase - 1, vectors[phase - 1], [members_here - 1])
        if phase < planes:
            members += [[(here, 0, seq)], [(new_x, 0, seq)], [(new_y, 0, seq)]]
        if phase < planes - 1 and phase not in leave:
            waiting = phase
        elif phase < planes - 1:
            projs += projected(phase, vectors[phase], range(members_here - 1))

    last = [c for key in fresh for c in add_chunks(key)]
    plan = on(members[:early], planes - 1, base)
    plan += [
        (segments, first, (base, early * seq + row), here)
        for segments, first, (_, row), here in on(members[early:-1], planes - 1, base, 0)
    ]
    plan += on(members[-1:], 0, None, len(members) - 1 - early)
    sums = product(plan, seq, chunks + last, (), late, (head,))
    sums = sums.reshape(len(members), -1).sum(axis=1)

    ids = jnp.concatenate(group_ids)
    total = planes * CORES * members_here
    rewards = jnp.sum(
        jnp.where(ids[:, None] == jnp.arange(total, dtype=jnp.int32)[None, :], sums[:, None], 0.0),
        axis=0,
    ).reshape(1, total)
    rewards = (rewards + swap_in_plane(rewards, 1)) + (
        swap_in_plane(rewards, 2) + swap_in_plane(rewards, 3)
    )
    rewards = tree_sum([rewards] + [turn(rewards, s) for s in range(1, planes)])
    own = own_scores(rewards, swap_core(rewards), pop_index * members_here, members_here, seq)
    return new_gate, new_up, own


def solution(mesh):
    n_pop, n_mp = mesh.shape["pop"], mesh.shape["mp"]
    planes = n_pop // CORES

    def shards(prompts, gate_weight, *rest):
        members_here, seq, width = prompts.shape
        own_cols = gate_weight.shape[1]
        gathered = 2 * width * own_cols + members_here * seq * width
        spread = 2 * width * own_cols // planes + planes * members_here * seq * width
        square = n_mp == 4 and members_here == n_mp and planes & (planes - 1) == 0
        if square and own_cols % (128 * planes) == 0 and spread < gathered:
            return spread_plan(planes, prompts, gate_weight, *rest)
        return gathered_plan(prompts, gate_weight, *rest)

    in_specs = (
        P("pop", None, None),
        P("pop", "mp"),
        P("pop", "mp"),
        P("mp"),
        P("pop"),
        P("pop"),
        P("pop"),
    )
    out_specs = (P("pop", "mp"), P("pop", "mp"), P("pop"))
    return jax.shard_map(shards, mesh=mesh, in_specs=in_specs, out_specs=out_specs, check_vma=False)
```

```python
import math

import jax
import jax.numpy as jnp
from jax import lax
from jax.experimental import pallas as pl
from jax.experimental.pallas import tpu as pltpu
from jax.sharding import PartitionSpec as P

sigma_perturb = 0.004
learn_rate = 0.0016
AXES = ("pop", "mp")
CORES = 2
SPARE_BYTES = 4 * 1024 * 1024


def shift_down(number, amount):
    return lax.shift_right_logical(number, jnp.full_like(number, amount))


def mix_bits(number):
    number = number ^ shift_down(number, 16)
    number = number * 2146121005
    number = number ^ shift_down(number, 15)
    number = number * -2073254261
    return number ^ shift_down(number, 16)


def factor_rows(seed_list, counter_list, slot, positions):
    anchor = mix_bits(
        seed_list * 1103515245 + mix_bits(counter_list * 668265263 + slot * 374761393)
    )
    hashed = mix_bits(anchor[:, None] + positions[None, :] * -1640531535)
    uniform_part = shift_down(hashed, 8).astype(jnp.float32) * (1.0 / 16777216.0)
    return (2.0 * uniform_part - 1.0 + 1.0 / 16777216.0) * 1.7320508075688772


def fresh_weights(gate_weight, up_weight, seeds, counters, ranks, row_start, column_ids):
    members_all = seeds.shape[0]
    fitness = (ranks.astype(jnp.float32) + 0.5) / members_all - 0.5
    scaling = learn_rate / (members_all * sigma_perturb)
    row_ids = row_start + jnp.arange(gate_weight.shape[0], dtype=jnp.int32)

    def fresh(weight, slot):
        right = factor_rows(seeds, counters, slot + 1, column_ids).astype(jnp.bfloat16)
        left = (factor_rows(seeds, counters, slot, row_ids) * fitness[:, None]).astype(jnp.bfloat16)
        update = scaling * jnp.dot(left.T, right, preferred_element_type=jnp.float32)
        return (weight.astype(jnp.float32) + update).astype(jnp.bfloat16)

    return fresh(gate_weight, 0), fresh(up_weight, 2)


def normalized(rewards):
    reward_mean = jnp.mean(rewards)
    reward_var = jnp.mean((rewards - reward_mean) ** 2)
    return (rewards - reward_mean) / jnp.sqrt(reward_var + 1e-05)


def gathered_plan(
    prompts, gate_weight, up_weight, reward_head, member_seeds, counters, member_ranks
):
    members_here, seq_len, width = prompts.shape
    own_rows, own_cols = gate_weight.shape
    pop_index = lax.axis_index("pop")
    column_ids = lax.axis_index("mp") * own_cols + jnp.arange(own_cols, dtype=jnp.int32)
    small = lax.all_gather(
        jnp.stack([member_seeds, counters, member_ranks]), "pop", axis=1, tiled=True
    )
    new_gate, new_up = fresh_weights(
        gate_weight, up_weight, small[0], small[1], small[2], pop_index * own_rows, column_ids
    )
    flat_rows = prompts.reshape(members_here * seq_len, width)
    later = counters + 1
    positions = jnp.arange(width, dtype=jnp.int32)

    def projected(weight, slot):
        base = jnp.dot(
            flat_rows,
            lax.all_gather(weight, "pop", axis=0, tiled=True),
            preferred_element_type=jnp.float32,
        ).reshape(members_here, seq_len, own_cols)
        vector = factor_rows(member_seeds, later, slot, positions).astype(jnp.bfloat16)
        column = factor_rows(member_seeds, later, slot + 1, column_ids)
        proj = jnp.einsum("mld,md->ml", prompts, vector, preferred_element_type=jnp.float32)
        return base + sigma_perturb * proj[:, :, None] * column[:, None, :]

    hidden = (jax.nn.silu(projected(new_gate, 0)) * projected(new_up, 2)).astype(jnp.bfloat16)
    partial = jnp.einsum("mlf,f->m", hidden, reward_head, preferred_element_type=jnp.float32)
    rewards = lax.all_gather(lax.psum(partial, "mp"), "pop", axis=0, tiled=True) / seq_len
    own = lax.dynamic_slice_in_dim(normalized(rewards), pop_index * members_here, members_here)
    return new_gate, new_up, own


def product_kernel(plan, counts, plane_of, seq, ranked, vectored, read_out, starts_ref, *refs):
    refs = list(refs)
    x_refs, w_refs, base_refs = [[refs.pop(0) for _ in range(count)] for count in counts]
    if ranked:
        proj_ref, col_ref = refs.pop(0), refs.pop(0)
    if vectored:
        vector_ref, vector_col_ref = refs.pop(0), refs.pop(0)
    if read_out:
        head_ref = refs.pop(0)
        head = head_ref[...].astype(jnp.float32)
    out_ref, weights = refs.pop(0), refs.pop(0)
    rows, totals = [], []
    for _, _, base, _ in plan:
        rows.append(refs.pop(0))
        totals.append(refs.pop(0) if base is not None or not read_out else None)
    row_sems, weight_sems, total_sems = refs
    columns = weights.shape[2]
    n_planes = 1 + plane_of[-1]
    plane_rows = weights.shape[1] // n_planes
    weight_copies = []
    for k, w_ref in enumerate(w_refs):
        depth = w_ref.shape[1]
        at = plane_of[k] * plane_rows + pl.multiple_of(starts_ref[len(w_refs) + k], depth)
        weight_copies.append(pltpu.make_async_copy(w_ref, weights.at[:, pl.ds(at, depth)], weight_sems.at[k]))
    group_copies = []
    for g, (segments, first, base, _) in enumerate(plan):
        copies = []
        row = 0
        for i, (x, start_row, count) in enumerate(segments):
            for plane in range(first, n_planes):
                start = pl.multiple_of(starts_ref[plane_of.index(plane)], plane_rows)
                copies.append(
                    pltpu.make_async_copy(
                        x_refs[x].at[pl.ds(start_row, count), pl.ds(start, plane_rows)],
                        rows[g].at[pl.ds(row, count), pl.ds((plane - first) * plane_rows, plane_rows)],
                        row_sems.at[g, i, plane],
                    )
                )
            row += count
        if base is not None:
            source = base_refs[base[0]].at[pl.ds(base[1], row)]
            copies.append(pltpu.make_async_copy(source, totals[g], total_sems.at[g]))
        group_copies.append(copies)
    taken, stages = set(), []
    for g, (_, first, _, _) in enumerate(plan):
        fresh = [k for k in range(len(w_refs)) if plane_of[k] >= first and k not in taken]
        taken.update(fresh)
        stages.append([weight_copies[k] for k in fresh] + group_copies[g])
    queue = list(stages)

    def start_stages(count):
        for copy in [c for stage in queue[:count] for c in stage]:
            copy.start()
        del queue[:count]

    start_stages(2 if read_out else 1)
    done_rows, out_copies = 0, []
    for g, (_, first, base, own_vectors) in enumerate(plan):
        for copy in stages[g]:
            copy.wait()
        start_stages(1 if read_out else 2)
        count = rows[g].shape[0]
        values = [
            jnp.dot(rows[g][...], weights[part, first * plane_rows :], preferred_element_type=jnp.float32)
            for part in range(2)
        ]
        for i in range(count // seq):
            here = slice(i * seq, (i + 1) * seq)
            there = slice(done_rows + i * seq, done_rows + (i + 1) * seq)
            member = done_rows // seq + i
            found = []
            vector = None
            for plane in range(first, n_planes if own_vectors is not None else first):
                start = pl.multiple_of(starts_ref[plane_of.index(plane)], plane_rows)
                term = lax.dot_general(
                    rows[g][here, (plane - first) * plane_rows : (plane + 1 - first) * plane_rows],
                    vector_ref[own_vectors + i, :, pl.ds(start, plane_rows)],
                    (((1,), (1,)), ((), ())),
                    preferred_element_type=jnp.float32,
                )
                vector = term if vector is None else vector + term
            for part in range(2):
                at = slice(part * columns, (part + 1) * columns)
                value = values[part][here]
                if base is not None:
                    value += totals[g][here, at].astype(jnp.float32)
                if ranked and own_vectors is None:
                    value += sigma_perturb * proj_ref[there, part : part + 1] * col_ref[part, member : member + 1, :]
                if vector is not None:
                    value += sigma_perturb * vector[:, part : part + 1] * vector_col_ref[part, own_vectors + i]
                if not read_out:
                    totals[g][here, at] = value.astype(jnp.bfloat16)
                found.append(value)
            if read_out:
                gate, up = found
                half = 0.5 * gate
                hidden = (half + half * jnp.tanh(half)) * up
                out_ref[member] = jnp.sum(hidden.reshape(seq // 8, 8, columns), axis=0) * head
        if not read_out:
            target = out_ref.at[pl.ds(done_rows, count)]
            out_copies.append(pltpu.make_async_copy(totals[g], target, total_sems.at[g]))
            out_copies[-1].start()
        done_rows += count
    for copy in out_copies:
        copy.wait()


def product(groups, seq, chunks, ranks=(), vectors=(), read_out=()):
    columns = chunks[0][3].shape[2]
    arrays, base_arrays, plan = [], [], []

    def number(array, known):
        for i, other in enumerate(known):
            if other is array:
                return i
        known.append(array)
        return len(known) - 1

    for segments, first, base, own_vectors in groups:
        placed = [(number(a, arrays), row, rows) for a, row, rows in segments]
        plan.append((placed, first, base and (number(base[0], base_arrays), base[1]), own_vectors))
    sizes = [sum(rows for _, _, rows in segments) for segments, _, _, _ in groups]
    total = sum(sizes)
    keys = list(dict.fromkeys(key for key, _, _, _ in chunks))
    plane_of = [keys.index(key) for key, _, _, _ in chunks]
    plane_rows = sum(chunk.shape[1] for key, _, _, chunk in chunks if key == keys[0])
    counts = [len(arrays), len(chunks), len(base_arrays)]
    buffers = [pltpu.VMEM((2, len(keys) * plane_rows, columns), jnp.bfloat16)]
    for (_, first, base, _), size in zip(groups, sizes):
        buffers.append(pltpu.VMEM((size, (len(keys) - first) * plane_rows), jnp.bfloat16))
        if base is not None or not read_out:
            buffers.append(pltpu.VMEM((size, 2 * columns), jnp.bfloat16))
    far = [pltpu.with_memory_space_constraint(a, pltpu.HBM) for a in [*arrays, *base_arrays]]
    near = [chunk for _, _, _, chunk in chunks]
    near[::2] = [pltpu.with_memory_space_constraint(a, pltpu.HBM) for a in near[::2]]
    near[-1] = pltpu.with_memory_space_constraint(near[-1], pltpu.VMEM)
    given = [*far[: len(arrays)], *near, *far[len(arrays) :]]
    extra = [*ranks, *vectors, *read_out]
    held = sum(2 * math.prod(b.shape) for b in buffers) + 4 * total * columns
    held += sum(4 * 128 * a.size // min(128, a.shape[-1]) for a in extra)
    vmem = pl.BlockSpec(memory_space=pltpu.VMEM)
    outside = pl.BlockSpec(memory_space=pl.ANY)
    shape = pltpu.HBM((total, 2 * columns), jnp.bfloat16)
    if read_out:
        shape = jax.ShapeDtypeStruct((total // seq, 8, columns), jnp.float32)
    parts = max(len(segments) for segments, _, _, _ in groups)
    return pl.pallas_call(
        lambda *refs: product_kernel(plan, counts, plane_of, seq, bool(ranks), bool(vectors), bool(read_out), *refs),
        out_shape=shape,
        in_specs=[pl.BlockSpec(memory_space=pltpu.SMEM)] + [outside] * len(given) + [vmem] * len(extra),
        out_specs=vmem if read_out else outside,
        scratch_shapes=[
            *buffers,
            pltpu.SemaphoreType.DMA((len(groups), parts, len(keys))),
            pltpu.SemaphoreType.DMA((len(chunks),)),
            pltpu.SemaphoreType.DMA((len(groups),)),
        ],
        compiler_params=pltpu.CompilerParams(vmem_limit_bytes=held + SPARE_BYTES),
        cost_estimate=pl.CostEstimate(flops=1, bytes_accessed=1, transcendentals=0),
    )(jnp.stack([c[1] for c in chunks] + [c[2] for c in chunks]), *given, *extra)


def tree_sum(terms):
    while len(terms) > 1:
        half = len(terms) // 2
        terms = [terms[i] + terms[i + half] for i in range(half)]
    return terms[0]


def own_scores(first, second, start, count, seq):
    def kernel(start_ref, first_ref, second_ref, out_ref):
        rewards = (first_ref[...] + second_ref[...]) / seq
        total = rewards.shape[1]
        mean = jnp.sum(rewards, axis=1, keepdims=True) / total
        spread = jnp.sum((rewards - mean) ** 2, axis=1, keepdims=True) / total
        scores = (rewards - mean) / jnp.sqrt(spread + 1e-05)
        places = lax.broadcasted_iota(jnp.int32, (count, total), 1)
        wanted = start_ref[0] + lax.broadcasted_iota(jnp.int32, (count, total), 0)
        column = jnp.sum(jnp.where(places == wanted, scores, 0.0), axis=1, keepdims=True)
        row, lane = [lax.broadcasted_iota(jnp.int32, (count, count), axis) for axis in range(2)]
        out_ref[...] = jnp.sum(jnp.where(row == lane, column, 0.0), axis=0, keepdims=True)

    vmem = pl.BlockSpec(memory_space=pltpu.VMEM)
    return pl.pallas_call(
        kernel,
        out_shape=jax.ShapeDtypeStruct((1, count), jnp.float32),
        in_specs=[pl.BlockSpec(memory_space=pltpu.SMEM), vmem, vmem],
        out_specs=vmem,
    )(start.reshape(1), *[pltpu.with_memory_space_constraint(a, pltpu.VMEM) for a in (first, second)]).reshape(count)


def spread_plan(planes, prompts, gate_weight, up_weight, reward_head, member_seeds, counters, member_ranks):
    members_here, seq, width = prompts.shape
    own_rows, own_cols = gate_weight.shape
    n_mp = members_here
    pop_index = lax.axis_index("pop")
    mp_index = lax.axis_index("mp")
    z, core = pop_index // CORES, pop_index % CORES
    block = own_cols // planes

    def pairs(move, keep=lambda z: True):
        out = []
        for a in range(planes):
            for c in range(CORES):
                for m in range(n_mp):
                    target = move(a, c, m)
                    if keep(a) and 0 <= target[0] < planes:
                        source = (a * CORES + c) * n_mp + m
                        out.append((source, (target[0] * CORES + target[1]) * n_mp + target[2]))
        return out

    def send(value, move, keep=lambda z: True):
        return lax.ppermute(value, AXES, pairs(move, keep))

    def swap_core(value):
        return send(value, lambda a, c, m: (a, 1 - c, m))

    def swap_in_plane(value, bit):
        return send(value, lambda a, c, m: (a, c, m ^ bit))

    def turn(value, s):
        return send(value, lambda a, c, m: ((a + s) % planes, c, m))

    def tie(*values):
        return lax.optimization_barrier(values)

    def up(value, s):
        return send(value, lambda a, c, m: (a + 1, c, m), lambda a: a >= s - 1)

    def down(value, s):
        return send(value, lambda a, c, m: (a - 1, c, m), lambda a: a <= planes - s)

    arrivals = []
    for a in range(planes):
        order = []
        for s in range(1, planes):
            if a - s >= 0:
                order.append((0, s, a - s))
            if a + s < planes:
                order.append((1, s, a + s))
        arrivals.append(order)

    def by_plane(numbers):
        value = jnp.int32(numbers[0])
        for a in range(1, planes):
            value = jnp.where(z == a, numbers[a], value)
        return value

    def round_block(r):
        picks = {}
        for a in range(planes):
            picks.setdefault(arrivals[a][r - 1][:2], []).append(a)
        chosen = None
        for (way, s), where in picks.items():
            here = z == where[0]
            for a in where[1:]:
                here = here | (z == a)
            value = hops[way][s]
            chosen = value if chosen is None else jnp.where(here, value, chosen)
        return chosen

    def piece(weights, s, first, count):
        corner = (first, (z + s) % planes * block)
        return jnp.stack([lax.dynamic_slice(w, corner, (count, block)) for w in weights])

    small = jnp.stack([member_seeds, counters, member_ranks])
    own_member = lax.dynamic_index_in_dim(prompts, mp_index, 0, keepdims=False)
    own_member, small = tie(own_member, small)
    hops = [[own_member, up(own_member, 1)], [own_member, down(own_member, 1)]]
    small_here = jnp.stack([small] + [turn(small, s) for s in range(1, planes)])
    small_other = swap_core(small_here)
    every = jnp.concatenate([small_here, small_other]).transpose(1, 0, 2).reshape(3, -1)
    head = lax.dynamic_slice_in_dim(reward_head, z * block, block).reshape(1, block)
    my_columns = mp_index * own_cols + z * block + jnp.arange(block, dtype=jnp.int32)
    positions = jnp.arange(width, dtype=jnp.int32)
    lanes = jnp.arange(members_here, dtype=jnp.int32)

    rel = mp_index ^ lanes
    rel_hot = (rel[:, None] == lanes[None, :]).astype(jnp.int32)
    flat = prompts.reshape(members_here * seq, width)
    members = [[(flat, i * seq, seq)] for i in range(members_here)]
    group_ids = [pop_index * members_here + lanes]
    picked = [(member_seeds, counters)]
    for r in range(1, planes):
        source = by_plane([arrivals[a][r - 1][2] for a in range(planes)])
        back = (z - source) % planes
        chosen = jnp.int32(0)
        for s in range(1, planes):
            chosen = jnp.where(back == s, small_here[s], chosen)
        chosen = jnp.sum(rel_hot[None] * chosen[:, None, :], axis=2)
        picked.append((chosen[0], chosen[1]))
        group_ids.append((source * CORES + core) * members_here + rel)

    def new_vectors(r):
        seeds, counts = picked[r]
        return jnp.stack(
            [factor_rows(seeds, counts + 1, slot, positions).astype(jnp.bfloat16) for slot in (0, 2)],
            axis=1,
        )

    def on_vector(rows, vector):
        return lax.dot_general(
            rows, vector, (((1,), (1,)), ((), ())), preferred_element_type=jnp.float32
        )

    def projected(r, vectors, some):
        found = []
        for i in some:
            parts = [
                on_vector(array[first : first + rows], vectors[i])
                for array, first, rows in members[r * members_here + i]
            ]
            found.append(parts[0] if len(parts) == 1 else jnp.concatenate(parts))
        return found

    cols = [
        jnp.stack([factor_rows(seeds, counts + 1, slot + 1, my_columns) for slot in (0, 2)])
        for seeds, counts in picked
    ]
    cols = jnp.concatenate(cols, axis=1)
    vectors = [new_vectors(r) for r in range(planes)]
    late_vectors = jnp.concatenate([vectors[planes - 2][members_here - 1 :], vectors[planes - 1]])
    late_vectors = jnp.pad(late_vectors, ((0, 0), (0, 14), (0, 0)))
    late = (late_vectors, cols[:, (planes - 1) * members_here - 1 :, None])
    projs = projected(0, vectors[0], range(members_here))

    column_ids = mp_index * own_cols + jnp.arange(own_cols, dtype=jnp.int32)
    weights = fresh_weights(
        gate_weight, up_weight, every[0], every[1], every[2], pop_index * own_rows, column_ids
    )
    new_gate, new_up = weights
    far_first = sorted(range(1, planes), key=lambda s: (-min(s, planes - s), s))
    half_rows = own_rows // 2
    queue = [(s, 0, own_rows) for s in far_first[:-1]]
    queue += [(far_first[-1], first, half_rows) for first in (0, half_rows)]
    leave = {planes - 2: queue[:1], planes - 1: queue[1:-1], planes: queue[-1:]}
    outgoing = {key: piece(weights, *key) for key in queue}
    landed = {(0, 0, own_rows): piece(weights, 0, 0, own_rows)}
    chunks = []

    def add_chunks(key):
        s, first, _ = key
        start = (z - s) % planes * CORES * own_rows
        return [
            (s, start, core * own_rows + first, landed[key]),
            (s, start, (1 - core) * own_rows + first, swap_core(landed[key])),
        ]

    half = seq // 2
    fresh = [(0, 0, own_rows)]
    base, early, early_planes, waiting = None, 0, 0, 0

    def on(some, first, base=None, vectors=None):
        groups = []
        for i in range(0, len(some), members_here):
            segments = []
            for segment in [s for m in some[i : i + members_here] for s in m]:
                array, row, rows = segments[-1] if segments else (None, 0, 0)
                if array is segment[0] and row + rows == segment[1]:
                    segments[-1] = (array, row, rows + segment[2])
                else:
                    segments.append(segment)
            groups.append((segments, first, None if base is None else (base, i * seq), vectors if vectors is None else vectors + i))
        return groups

    hops[0][1], hops[1][1] = tie(hops[0][1], hops[1][1])
    to_x = to_y = next_here = round_block(1)
    for phase in range(1, planes + 1):
        if phase < planes - 1:
            hops[0].append(up(hops[0][phase], phase + 1))
            hops[1].append(down(hops[1][phase], phase + 1))
        if phase < planes:
            here = next_here
        new_x = swap_in_plane(to_x, 1)
        new_y = swap_in_plane(to_y, 2)
        for key in leave.get(phase, ()):
            landed[key] = turn(outgoing[key], key[0])
        new_chunks = [c for key in fresh for c in add_chunks(key)]
        fresh = leave.get(phase, ())
        known = chunks + new_chunks
        if phase == planes - 1:
            early, early_planes = len(members), len(set(c[0] for c in known))
            ranks = (jnp.concatenate(projs), cols[:, :early])
            base = product(on(members, 0), seq, known, ranks)
        elif phase == planes:
            landed_first = [c for c in chunks + new_chunks if c[0] != far_first[-1]]
            groups = on(members[:early], early_planes, base) + on(members[early:], 0, None, 0)
            base = product(groups, seq, landed_first, (), late)
        def next_sends():
            to_x, to_y, here = [new_y[:half]], [new_x[half:seq]], None
            if phase + 1 < planes:
                here = round_block(phase + 1)
                to_x, to_y = [here, *to_x], [here, *to_y]
            return jnp.concatenate(to_x), jnp.concatenate(to_y), here

        ahead = ()
        if phase in leave and phase < planes:
            held = [members[waiting * members_here + i][0][0] for i in range(members_here - 1) if waiting]
            hops, new_x, new_y, held = tie(hops, new_x, new_y, held)
            ahead = next_sends()
            projs += [on_vector(array, vectors[waiting][i]) for i, array in enumerate(held)]
            waiting = 0
        held = [chunk for _, _, _, chunk in new_chunks]
        parts = (hops, new_x, new_y, ahead, landed, held, outgoing, base, cols, late, projs, head)
        hops, new_x, new_y, ahead, landed, held, outgoing, base, cols, late, projs, head = tie(*parts)
        if phase < planes:
            to_x, to_y, next_here = ahead or next_sends()
        chunks += [(*c[:3], chunk) for c, chunk in zip(new_chunks, held)]
        if phase > 1:
            first = seq if phase < planes else 0
            members.append([(new_x, first, half), (new_y, first, half)])
        if 1 < phase < planes - 1:
            projs += projected(phase - 1, vectors[phase - 1], [members_here - 1])
        if phase < planes:
            members += [[(here, 0, seq)], [(new_x, 0, seq)], [(new_y, 0, seq)]]
        if phase < planes - 1 and phase not in leave:
            waiting = phase
        elif phase < planes - 1:
            projs += projected(phase, vectors[phase], range(members_here - 1))

    last = [c for key in fresh for c in add_chunks(key)]
    plan = on(members[:early], planes - 1, base)
    plan += [
        (segments, first, (base, early * seq + row), here)
        for segments, first, (_, row), here in on(members[early:-1], planes - 1, base, 0)
    ]
    plan += on(members[-1:], 0, None, len(members) - 1 - early)
    sums = product(plan, seq, chunks + last, (), late, (head,))
    sums = sums.reshape(len(members), -1).sum(axis=1)

    ids = jnp.concatenate(group_ids)
    total = planes * CORES * members_here
    rewards = jnp.sum(
        jnp.where(ids[:, None] == jnp.arange(total, dtype=jnp.int32)[None, :], sums[:, None], 0.0),
        axis=0,
    ).reshape(1, total)
    rewards = (rewards + swap_in_plane(rewards, 1)) + (
        swap_in_plane(rewards, 2) + swap_in_plane(rewards, 3)
    )
    rewards = tree_sum([rewards] + [turn(rewards, s) for s in range(1, planes)])
    own = own_scores(rewards, swap_core(rewards), pop_index * members_here, members_here, seq)
    return new_gate, new_up, own


def solution(mesh):
    n_pop, n_mp = mesh.shape["pop"], mesh.shape["mp"]
    planes = n_pop // CORES

    def shards(prompts, gate_weight, *rest):
        members_here, seq, width = prompts.shape
        own_cols = gate_weight.shape[1]
        gathered = 2 * width * own_cols + members_here * seq * width
        spread = 2 * width * own_cols // planes + planes * members_here * seq * width
        square = n_mp == 4 and members_here == n_mp and planes & (planes - 1) == 0
        if square and own_cols % (128 * planes) == 0 and spread < gathered:
            return spread_plan(planes, prompts, gate_weight, *rest)
        return gathered_plan(prompts, gate_weight, *rest)

    in_specs = (
        P("pop", None, None),
        P("pop", "mp"),
        P("pop", "mp"),
        P("mp"),
        P("pop"),
        P("pop"),
        P("pop"),
    )
    out_specs = (P("pop", "mp"), P("pop", "mp"), P("pop"))
    return jax.shard_map(shards, mesh=mesh, in_specs=in_specs, out_specs=out_specs, check_vma=False)
```

```python
import math

import jax
import jax.numpy as jnp
from jax import lax
from jax.experimental import pallas as pl
from jax.experimental.pallas import tpu as pltpu
from jax.sharding import PartitionSpec as P

sigma_perturb = 0.004
learn_rate = 0.0016
AXES = ("pop", "mp")
CORES = 2
SPARE_BYTES = 4 * 1024 * 1024


def shift_down(number, amount):
    return lax.shift_right_logical(number, jnp.full_like(number, amount))


def mix_bits(number):
    number = number ^ shift_down(number, 16)
    number = number * 2146121005
    number = number ^ shift_down(number, 15)
    number = number * -2073254261
    return number ^ shift_down(number, 16)


def factor_rows(seed_list, counter_list, slot, positions):
    anchor = mix_bits(
        seed_list * 1103515245 + mix_bits(counter_list * 668265263 + slot * 374761393)
    )
    hashed = mix_bits(anchor[:, None] + positions[None, :] * -1640531535)
    uniform_part = shift_down(hashed, 8).astype(jnp.float32) * (1.0 / 16777216.0)
    return (2.0 * uniform_part - 1.0 + 1.0 / 16777216.0) * 1.7320508075688772


def fresh_weights(gate_weight, up_weight, seeds, counters, ranks, row_start, column_ids):
    members_all = seeds.shape[0]
    fitness = (ranks.astype(jnp.float32) + 0.5) / members_all - 0.5
    scaling = learn_rate / (members_all * sigma_perturb)
    row_ids = row_start + jnp.arange(gate_weight.shape[0], dtype=jnp.int32)

    def fresh(weight, slot):
        right = factor_rows(seeds, counters, slot + 1, column_ids).astype(jnp.bfloat16)
        left = (factor_rows(seeds, counters, slot, row_ids) * fitness[:, None]).astype(jnp.bfloat16)
        update = scaling * jnp.dot(left.T, right, preferred_element_type=jnp.float32)
        return (weight.astype(jnp.float32) + update).astype(jnp.bfloat16)

    return fresh(gate_weight, 0), fresh(up_weight, 2)


def normalized(rewards):
    reward_mean = jnp.mean(rewards)
    reward_var = jnp.mean((rewards - reward_mean) ** 2)
    return (rewards - reward_mean) / jnp.sqrt(reward_var + 1e-05)


def gathered_plan(
    prompts, gate_weight, up_weight, reward_head, member_seeds, counters, member_ranks
):
    members_here, seq_len, width = prompts.shape
    own_rows, own_cols = gate_weight.shape
    pop_index = lax.axis_index("pop")
    column_ids = lax.axis_index("mp") * own_cols + jnp.arange(own_cols, dtype=jnp.int32)
    small = lax.all_gather(
        jnp.stack([member_seeds, counters, member_ranks]), "pop", axis=1, tiled=True
    )
    new_gate, new_up = fresh_weights(
        gate_weight, up_weight, small[0], small[1], small[2], pop_index * own_rows, column_ids
    )
    flat_rows = prompts.reshape(members_here * seq_len, width)
    later = counters + 1
    positions = jnp.arange(width, dtype=jnp.int32)

    def projected(weight, slot):
        base = jnp.dot(
            flat_rows,
            lax.all_gather(weight, "pop", axis=0, tiled=True),
            preferred_element_type=jnp.float32,
        ).reshape(members_here, seq_len, own_cols)
        vector = factor_rows(member_seeds, later, slot, positions).astype(jnp.bfloat16)
        column = factor_rows(member_seeds, later, slot + 1, column_ids)
        proj = jnp.einsum("mld,md->ml", prompts, vector, preferred_element_type=jnp.float32)
        return base + sigma_perturb * proj[:, :, None] * column[:, None, :]

    hidden = (jax.nn.silu(projected(new_gate, 0)) * projected(new_up, 2)).astype(jnp.bfloat16)
    partial = jnp.einsum("mlf,f->m", hidden, reward_head, preferred_element_type=jnp.float32)
    rewards = lax.all_gather(lax.psum(partial, "mp"), "pop", axis=0, tiled=True) / seq_len
    own = lax.dynamic_slice_in_dim(normalized(rewards), pop_index * members_here, members_here)
    return new_gate, new_up, own


def product_kernel(plan, counts, plane_of, seq, ranked, vectored, read_out, starts_ref, *refs):
    refs = list(refs)
    x_refs, w_refs, base_refs = [[refs.pop(0) for _ in range(count)] for count in counts]
    if ranked:
        proj_ref, col_ref = refs.pop(0), refs.pop(0)
    if vectored:
        vector_ref, vector_col_ref = refs.pop(0), refs.pop(0)
    if read_out:
        head_ref = refs.pop(0)
        head = head_ref[...].astype(jnp.float32)
    out_ref, weights = refs.pop(0), refs.pop(0)
    rows, totals = [], []
    for _, _, base, _ in plan:
        rows.append(refs.pop(0))
        totals.append(refs.pop(0) if base is not None or not read_out else None)
    row_sems, weight_sems, total_sems = refs
    columns = weights.shape[2]
    n_planes = 1 + plane_of[-1]
    plane_rows = weights.shape[1] // n_planes
    weight_copies = []
    for k, w_ref in enumerate(w_refs):
        depth = w_ref.shape[1]
        at = plane_of[k] * plane_rows + pl.multiple_of(starts_ref[len(w_refs) + k], depth)
        weight_copies.append(pltpu.make_async_copy(w_ref, weights.at[:, pl.ds(at, depth)], weight_sems.at[k]))
    group_copies = []
    for g, (segments, first, base, _) in enumerate(plan):
        copies = []
        row = 0
        for i, (x, start_row, count) in enumerate(segments):
            for plane in range(first, n_planes):
                start = pl.multiple_of(starts_ref[plane_of.index(plane)], plane_rows)
                copies.append(
                    pltpu.make_async_copy(
                        x_refs[x].at[pl.ds(start_row, count), pl.ds(start, plane_rows)],
                        rows[g].at[pl.ds(row, count), pl.ds((plane - first) * plane_rows, plane_rows)],
                        row_sems.at[g, i, plane],
                    )
                )
            row += count
        if base is not None:
            source = base_refs[base[0]].at[pl.ds(base[1], row)]
            copies.append(pltpu.make_async_copy(source, totals[g], total_sems.at[g]))
        group_copies.append(copies)
    taken, stages = set(), []
    for g, (_, first, _, _) in enumerate(plan):
        fresh = [k for k in range(len(w_refs)) if plane_of[k] >= first and k not in taken]
        taken.update(fresh)
        stages.append([weight_copies[k] for k in fresh] + group_copies[g])
    queue = list(stages)

    def start_stages(count):
        for copy in [c for stage in queue[:count] for c in stage]:
            copy.start()
        del queue[:count]

    start_stages(2 if read_out else 1)
    done_rows, out_copies = 0, []
    for g, (_, first, base, own_vectors) in enumerate(plan):
        for copy in stages[g]:
            copy.wait()
        start_stages(1 if read_out else 2)
        count = rows[g].shape[0]
        values = [
            jnp.dot(rows[g][...], weights[part, first * plane_rows :], preferred_element_type=jnp.float32)
            for part in range(2)
        ]
        for i in range(count // seq):
            here = slice(i * seq, (i + 1) * seq)
            there = slice(done_rows + i * seq, done_rows + (i + 1) * seq)
            member = done_rows // seq + i
            found = []
            vector = None
            for plane in range(first, n_planes if own_vectors is not None else first):
                start = pl.multiple_of(starts_ref[plane_of.index(plane)], plane_rows)
                term = lax.dot_general(
                    rows[g][here, (plane - first) * plane_rows : (plane + 1 - first) * plane_rows],
                    vector_ref[own_vectors + i, :, pl.ds(start, plane_rows)],
                    (((1,), (1,)), ((), ())),
                    preferred_element_type=jnp.float32,
                )
                vector = term if vector is None else vector + term
            for part in range(2):
                at = slice(part * columns, (part + 1) * columns)
                value = values[part][here]
                if base is not None:
                    value += totals[g][here, at].astype(jnp.float32)
                if ranked and own_vectors is None:
                    value += sigma_perturb * proj_ref[there, part : part + 1] * col_ref[part, member : member + 1, :]
                if vector is not None:
                    value += sigma_perturb * vector[:, part : part + 1] * vector_col_ref[part, own_vectors + i]
                if not read_out:
                    totals[g][here, at] = value.astype(jnp.bfloat16)
                found.append(value)
            if read_out:
                gate, up = found
                half = 0.5 * gate
                hidden = (half + half * jnp.tanh(half)) * up
                out_ref[member] = jnp.sum(hidden.reshape(seq // 8, 8, columns), axis=0) * head
        if not read_out:
            target = out_ref.at[pl.ds(done_rows, count)]
            out_copies.append(pltpu.make_async_copy(totals[g], target, total_sems.at[g]))
            out_copies[-1].start()
        done_rows += count
    for copy in out_copies:
        copy.wait()


def product(groups, seq, chunks, ranks=(), vectors=(), read_out=()):
    columns = chunks[0][3].shape[2]
    arrays, base_arrays, plan = [], [], []

    def number(array, known):
        for i, other in enumerate(known):
            if other is array:
                return i
        known.append(array)
        return len(known) - 1

    for segments, first, base, own_vectors in groups:
        placed = [(number(a, arrays), row, rows) for a, row, rows in segments]
        plan.append((placed, first, base and (number(base[0], base_arrays), base[1]), own_vectors))
    sizes = [sum(rows for _, _, rows in segments) for segments, _, _, _ in groups]
    total = sum(sizes)
    keys = list(dict.fromkeys(key for key, _, _, _ in chunks))
    plane_of = [keys.index(key) for key, _, _, _ in chunks]
    plane_rows = sum(chunk.shape[1] for key, _, _, chunk in chunks if key == keys[0])
    counts = [len(arrays), len(chunks), len(base_arrays)]
    buffers = [pltpu.VMEM((2, len(keys) * plane_rows, columns), jnp.bfloat16)]
    for (_, first, base, _), size in zip(groups, sizes):
        buffers.append(pltpu.VMEM((size, (len(keys) - first) * plane_rows), jnp.bfloat16))
        if base is not None or not read_out:
            buffers.append(pltpu.VMEM((size, 2 * columns), jnp.bfloat16))
    far = [pltpu.with_memory_space_constraint(a, pltpu.HBM) for a in [*arrays, *base_arrays]]
    near = [chunk for _, _, _, chunk in chunks]
    near[::2] = [pltpu.with_memory_space_constraint(a, pltpu.HBM) for a in near[::2]]
    near[-1] = pltpu.with_memory_space_constraint(near[-1], pltpu.VMEM)
    given = [*far[: len(arrays)], *near, *far[len(arrays) :]]
    extra = [*ranks, *vectors, *read_out]
    held = sum(2 * math.prod(b.shape) for b in buffers) + 4 * total * columns
    held += sum(4 * 128 * a.size // min(128, a.shape[-1]) for a in extra)
    vmem = pl.BlockSpec(memory_space=pltpu.VMEM)
    outside = pl.BlockSpec(memory_space=pl.ANY)
    shape = pltpu.HBM((total, 2 * columns), jnp.bfloat16)
    if read_out:
        shape = jax.ShapeDtypeStruct((total // seq, 8, columns), jnp.float32)
    parts = max(len(segments) for segments, _, _, _ in groups)
    return pl.pallas_call(
        lambda *refs: product_kernel(plan, counts, plane_of, seq, bool(ranks), bool(vectors), bool(read_out), *refs),
        out_shape=shape,
        in_specs=[pl.BlockSpec(memory_space=pltpu.SMEM)] + [outside] * len(given) + [vmem] * len(extra),
        out_specs=vmem if read_out else outside,
        scratch_shapes=[
            *buffers,
            pltpu.SemaphoreType.DMA((len(groups), parts, len(keys))),
            pltpu.SemaphoreType.DMA((len(chunks),)),
            pltpu.SemaphoreType.DMA((len(groups),)),
        ],
        compiler_params=pltpu.CompilerParams(vmem_limit_bytes=held + SPARE_BYTES),
        cost_estimate=pl.CostEstimate(flops=1, bytes_accessed=1, transcendentals=0),
    )(jnp.stack([c[1] for c in chunks] + [c[2] for c in chunks]), *given, *extra)


def tree_sum(terms):
    while len(terms) > 1:
        half = len(terms) // 2
        terms = [terms[i] + terms[i + half] for i in range(half)]
    return terms[0]


def own_scores(first, second, start, count, seq):
    def kernel(start_ref, first_ref, second_ref, out_ref):
        rewards = (first_ref[...] + second_ref[...]) / seq
        total = rewards.shape[1]
        mean = jnp.sum(rewards, axis=1, keepdims=True) / total
        spread = jnp.sum((rewards - mean) ** 2, axis=1, keepdims=True) / total
        scores = (rewards - mean) / jnp.sqrt(spread + 1e-05)
        places = lax.broadcasted_iota(jnp.int32, (count, total), 1)
        wanted = start_ref[0] + lax.broadcasted_iota(jnp.int32, (count, total), 0)
        column = jnp.sum(jnp.where(places == wanted, scores, 0.0), axis=1, keepdims=True)
        row, lane = [lax.broadcasted_iota(jnp.int32, (count, count), axis) for axis in range(2)]
        out_ref[...] = jnp.sum(jnp.where(row == lane, column, 0.0), axis=0, keepdims=True)

    vmem = pl.BlockSpec(memory_space=pltpu.VMEM)
    return pl.pallas_call(
        kernel,
        out_shape=jax.ShapeDtypeStruct((1, count), jnp.float32),
        in_specs=[pl.BlockSpec(memory_space=pltpu.SMEM), vmem, vmem],
        out_specs=vmem,
    )(start.reshape(1), *[pltpu.with_memory_space_constraint(a, pltpu.VMEM) for a in (first, second)]).reshape(count)


def spread_plan(planes, prompts, gate_weight, up_weight, reward_head, member_seeds, counters, member_ranks):
    members_here, seq, width = prompts.shape
    own_rows, own_cols = gate_weight.shape
    n_mp = members_here
    pop_index = lax.axis_index("pop")
    mp_index = lax.axis_index("mp")
    z, core = pop_index // CORES, pop_index % CORES
    block = own_cols // planes

    def pairs(move, keep=lambda z: True):
        out = []
        for a in range(planes):
            for c in range(CORES):
                for m in range(n_mp):
                    target = move(a, c, m)
                    if keep(a) and 0 <= target[0] < planes:
                        source = (a * CORES + c) * n_mp + m
                        out.append((source, (target[0] * CORES + target[1]) * n_mp + target[2]))
        return out

    def send(value, move, keep=lambda z: True):
        return lax.ppermute(value, AXES, pairs(move, keep))

    def swap_core(value):
        return send(value, lambda a, c, m: (a, 1 - c, m))

    def swap_in_plane(value, bit):
        return send(value, lambda a, c, m: (a, c, m ^ bit))

    def turn(value, s):
        return send(value, lambda a, c, m: ((a + s) % planes, c, m))

    def tie(*values):
        return lax.optimization_barrier(values)

    def up(value, s):
        return send(value, lambda a, c, m: (a + 1, c, m), lambda a: a >= s - 1)

    def down(value, s):
        return send(value, lambda a, c, m: (a - 1, c, m), lambda a: a <= planes - s)

    arrivals = []
    for a in range(planes):
        order = []
        for s in range(1, planes):
            if a - s >= 0:
                order.append((0, s, a - s))
            if a + s < planes:
                order.append((1, s, a + s))
        arrivals.append(order)

    def by_plane(numbers):
        value = jnp.int32(numbers[0])
        for a in range(1, planes):
            value = jnp.where(z == a, numbers[a], value)
        return value

    def round_block(r):
        picks = {}
        for a in range(planes):
            picks.setdefault(arrivals[a][r - 1][:2], []).append(a)
        chosen = None
        for (way, s), where in picks.items():
            here = z == where[0]
            for a in where[1:]:
                here = here | (z == a)
            value = hops[way][s]
            chosen = value if chosen is None else jnp.where(here, value, chosen)
        return chosen

    def piece(weights, s, first, count):
        corner = (first, (z + s) % planes * block)
        return jnp.stack([lax.dynamic_slice(w, corner, (count, block)) for w in weights])

    small = jnp.stack([member_seeds, counters, member_ranks])
    own_member = lax.dynamic_index_in_dim(prompts, mp_index, 0, keepdims=False)
    own_member, small = tie(own_member, small)
    hops = [[own_member, up(own_member, 1)], [own_member, down(own_member, 1)]]
    small_here = jnp.stack([small] + [turn(small, s) for s in range(1, planes)])
    small_other = swap_core(small_here)
    every = jnp.concatenate([small_here, small_other]).transpose(1, 0, 2).reshape(3, -1)
    head = lax.dynamic_slice_in_dim(reward_head, z * block, block).reshape(1, block)
    my_columns = mp_index * own_cols + z * block + jnp.arange(block, dtype=jnp.int32)
    positions = jnp.arange(width, dtype=jnp.int32)
    lanes = jnp.arange(members_here, dtype=jnp.int32)

    rel = mp_index ^ lanes
    rel_hot = (rel[:, None] == lanes[None, :]).astype(jnp.int32)
    flat = prompts.reshape(members_here * seq, width)
    members = [[(flat, i * seq, seq)] for i in range(members_here)]
    group_ids = [pop_index * members_here + lanes]
    picked = [(member_seeds, counters)]
    for r in range(1, planes):
        source = by_plane([arrivals[a][r - 1][2] for a in range(planes)])
        back = (z - source) % planes
        chosen = jnp.int32(0)
        for s in range(1, planes):
            chosen = jnp.where(back == s, small_here[s], chosen)
        chosen = jnp.sum(rel_hot[None] * chosen[:, None, :], axis=2)
        picked.append((chosen[0], chosen[1]))
        group_ids.append((source * CORES + core) * members_here + rel)

    def new_vectors(r):
        seeds, counts = picked[r]
        return jnp.stack(
            [factor_rows(seeds, counts + 1, slot, positions).astype(jnp.bfloat16) for slot in (0, 2)],
            axis=1,
        )

    def on_vector(rows, vector):
        return lax.dot_general(
            rows, vector, (((1,), (1,)), ((), ())), preferred_element_type=jnp.float32
        )

    def projected(r, vectors, some):
        found = []
        for i in some:
            parts = [
                on_vector(array[first : first + rows], vectors[i])
                for array, first, rows in members[r * members_here + i]
            ]
            found.append(parts[0] if len(parts) == 1 else jnp.concatenate(parts))
        return found

    cols = [
        jnp.stack([factor_rows(seeds, counts + 1, slot + 1, my_columns) for slot in (0, 2)])
        for seeds, counts in picked
    ]
    cols = jnp.concatenate(cols, axis=1)
    vectors = [new_vectors(r) for r in range(planes)]
    late_vectors = jnp.concatenate([vectors[planes - 2][members_here - 1 :], vectors[planes - 1]])
    late_vectors = jnp.pad(late_vectors, ((0, 0), (0, 14), (0, 0)))
    late = (late_vectors, cols[:, (planes - 1) * members_here - 1 :, None])
    projs = projected(0, vectors[0], range(members_here))

    column_ids = mp_index * own_cols + jnp.arange(own_cols, dtype=jnp.int32)
    weights = fresh_weights(
        gate_weight, up_weight, every[0], every[1], every[2], pop_index * own_rows, column_ids
    )
    new_gate, new_up = weights
    far_first = sorted(range(1, planes), key=lambda s: (-min(s, planes - s), s))
    half_rows = own_rows // 2
    queue = [(s, 0, own_rows) for s in far_first[:-1]]
    queue += [(far_first[-1], first, half_rows) for first in (0, half_rows)]
    leave = {planes - 2: queue[:1], planes - 1: queue[1:-1], planes: queue[-1:]}
    outgoing = {key: piece(weights, *key) for key in queue}
    landed = {(0, 0, own_rows): piece(weights, 0, 0, own_rows)}
    chunks = []

    def add_chunks(key):
        s, first, _ = key
        start = (z - s) % planes * CORES * own_rows
        return [
            (s, start, core * own_rows + first, landed[key]),
            (s, start, (1 - core) * own_rows + first, swap_core(landed[key])),
        ]

    half = seq // 2
    fresh = [(0, 0, own_rows)]
    base, early, early_planes, waiting = None, 0, 0, 0

    def on(some, first, base=None, vectors=None):
        groups = []
        for i in range(0, len(some), members_here):
            segments = []
            for segment in [s for m in some[i : i + members_here] for s in m]:
                array, row, rows = segments[-1] if segments else (None, 0, 0)
                if array is segment[0] and row + rows == segment[1]:
                    segments[-1] = (array, row, rows + segment[2])
                else:
                    segments.append(segment)
            groups.append((segments, first, None if base is None else (base, i * seq), vectors if vectors is None else vectors + i))
        return groups

    hops[0][1], hops[1][1] = tie(hops[0][1], hops[1][1])
    to_x = to_y = next_here = round_block(1)
    for phase in range(1, planes + 1):
        if phase < planes - 1:
            hops[0].append(up(hops[0][phase], phase + 1))
            hops[1].append(down(hops[1][phase], phase + 1))
        if phase < planes:
            here = next_here
        new_x = swap_in_plane(to_x, 1)
        new_y = swap_in_plane(to_y, 2)
        for key in leave.get(phase, ()):
            landed[key] = turn(outgoing[key], key[0])
        new_chunks = [c for key in fresh for c in add_chunks(key)]
        fresh = leave.get(phase, ())
        known = chunks + new_chunks
        if phase == planes - 1:
            early, early_planes = len(members), len(set(c[0] for c in known))
            ranks = (jnp.concatenate(projs), cols[:, :early])
            base = product(on(members, 0), seq, known, ranks)
        elif phase == planes:
            landed_first = [c for c in chunks + new_chunks if c[0] != far_first[-1]]
            groups = on(members[:early], early_planes, base) + on(members[early:], 0, None, 0)
            base = product(groups, seq, landed_first, (), late)
        def next_sends():
            to_x, to_y, here = [new_y[:half]], [new_x[half:seq]], None
            if phase + 1 < planes:
                here = round_block(phase + 1)
                to_x, to_y = [here, *to_x], [here, *to_y]
            return jnp.concatenate(to_x), jnp.concatenate(to_y), here

        ahead = ()
        if phase in leave and phase < planes:
            held = [members[waiting * members_here + i][0][0] for i in range(members_here - 1) if waiting]
            hops, new_x, new_y, held = tie(hops, new_x, new_y, held)
            ahead = next_sends()
            projs += [on_vector(array, vectors[waiting][i]) for i, array in enumerate(held)]
            waiting = 0
        held = [chunk for _, _, _, chunk in new_chunks]
        parts = (hops, new_x, new_y, ahead, landed, held, outgoing, base, cols, late, projs, head)
        hops, new_x, new_y, ahead, landed, held, outgoing, base, cols, late, projs, head = tie(*parts)
        if phase < planes:
            to_x, to_y, next_here = ahead or next_sends()
        chunks += [(*c[:3], chunk) for c, chunk in zip(new_chunks, held)]
        if phase > 1:
            first = seq if phase < planes else 0
            members.append([(new_x, first, half), (new_y, first, half)])
        if 1 < phase < planes - 1:
            projs += projected(phase - 1, vectors[phase - 1], [members_here - 1])
        if phase < planes:
            members += [[(here, 0, seq)], [(new_x, 0, seq)], [(new_y, 0, seq)]]
        if phase < planes - 1 and phase not in leave:
            waiting = phase
        elif phase < planes - 1:
            projs += projected(phase, vectors[phase], range(members_here - 1))

    last = [c for key in fresh for c in add_chunks(key)]
    plan = on(members[:early], planes - 1, base)
    plan += [
        (segments, first, (base, early * seq + row), here)
        for segments, first, (_, row), here in on(members[early:-1], planes - 1, base, 0)
    ]
    plan += on(members[-1:], 0, None, len(members) - 1 - early)
    sums = product(plan, seq, chunks + last, (), late, (head,))
    sums = sums.reshape(len(members), -1).sum(axis=1)

    ids = jnp.concatenate(group_ids)
    total = planes * CORES * members_here
    rewards = jnp.sum(
        jnp.where(ids[:, None] == jnp.arange(total, dtype=jnp.int32)[None, :], sums[:, None], 0.0),
        axis=0,
    ).reshape(1, total)
    rewards = tree_sum([rewards] + [turn(rewards, s) for s in range(1, planes)])
    rewards = (rewards + swap_in_plane(rewards, 1)) + (
        swap_in_plane(rewards, 2) + swap_in_plane(rewards, 3)
    )
    own = own_scores(rewards, swap_core(rewards), pop_index * members_here, members_here, seq)
    return new_gate, new_up, own


def solution(mesh):
    n_pop, n_mp = mesh.shape["pop"], mesh.shape["mp"]
    planes = n_pop // CORES

    def shards(prompts, gate_weight, *rest):
        members_here, seq, width = prompts.shape
        own_cols = gate_weight.shape[1]
        gathered = 2 * width * own_cols + members_here * seq * width
        spread = 2 * width * own_cols // planes + planes * members_here * seq * width
        square = n_mp == 4 and members_here == n_mp and planes & (planes - 1) == 0
        if square and own_cols % (128 * planes) == 0 and spread < gathered:
            return spread_plan(planes, prompts, gate_weight, *rest)
        return gathered_plan(prompts, gate_weight, *rest)

    in_specs = (
        P("pop", None, None),
        P("pop", "mp"),
        P("pop", "mp"),
        P("mp"),
        P("pop"),
        P("pop"),
        P("pop"),
    )
    out_specs = (P("pop", "mp"), P("pop", "mp"), P("pop"))
    return jax.shard_map(shards, mesh=mesh, in_specs=in_specs, out_specs=out_specs, check_vma=False)
```
